32 devices in a mesh: slab: 4 (over z), tile: 8 (over y, x, core).
Axes of the slice: x: 2, y: 2, z: 4, core: 2. Of those that a mesh axis runs over, the one named last changes fastest.
Arguments:
- features: bfloat16 [256, 64, 512], P(('slab', 'tile')), may hold values from -6 to 6
- cotangent: bfloat16 [256, 64, 512], P(('slab', 'tile')), may hold values from -6 to 6
- weight: bfloat16 [64, 1728], replicated, may hold values from -0.15625 to 0.15625
- block_table: int32 [4, 16, 8], replicated, may hold values from -1 to 7, as said below
Outputs:
- conv_out: bfloat16 [256, 64, 512], P(('slab', 'tile'))
- grad_features: bfloat16 [256, 64, 512], P(('slab', 'tile'))
- grad_weight: float32 [64, 1728], replicated
The draws below stay inside these ranges and needn't reach their ends.
Inputs may be any that keep to these rules, and one draw needn't show every extreme that they name: `block_table`: -1 marks an inactive block. An active block (bz, by, bx) holds (by modulo 2) * 4 plus the number of active blocks before it along x in its row (bz, by). Every row has at least one and at most 4 active blocks; all rows of one block layer bz share an active block in one column. Some row with by modulo 2 = 1 has exactly 4.
All inputs are finite; a program needn't handle non-finite values.
Results may differ from the reference program's by a relative error of at most 0.001.
Values may be sent and summed in bfloat16 or wider, within the bound.
A program may use at most 64 MiB of HBM per device.

```python
import jax
import jax.numpy as jnp
from jax import lax

CH = 64
LZ = 1
YR = 2
LX = 8
CAPL = 4
BLOCKS = 256
ZBLOCKS = 4
YBLOCKS = 16
N_TILE = 8


def draw_block_table(key, part):
    row_count = ZBLOCKS * YBLOCKS
    key_count, key_slab, key_tile, key_order, key_column = jax.random.split(key, 5)
    counts = jax.random.randint(key_count, (row_count,), 1, CAPL + 1)
    full_slab = jax.random.randint(key_slab, (), 0, ZBLOCKS // LZ)
    full_tile = jax.random.randint(key_tile, (), 0, YBLOCKS // YR)
    full_row = (full_slab * LZ + LZ - 1) * YBLOCKS + full_tile * YR + YR - 1
    row_ids = jnp.arange(row_count).astype(jnp.int32)
    counts = jnp.where(row_ids == full_row, CAPL, counts)
    order_keys = jax.random.split(key_order, row_count)
    ranking = jax.vmap(lambda row_key: jax.random.permutation(row_key, LX))(order_keys)
    layer_column = jax.random.randint(key_column, (ZBLOCKS,), 0, LX)
    row_column = layer_column[row_ids // YBLOCKS]
    positions = jnp.arange(LX).astype(jnp.int32)
    rank_there = jnp.sum(jnp.where(positions[None, :] == row_column[:, None], ranking, 0), axis=1)
    lifted = jnp.where(ranking < rank_there[:, None], ranking + 1, ranking)
    ranking = jnp.where(positions[None, :] == row_column[:, None], 0, lifted)
    active = (ranking < counts[:, None]).astype(jnp.int32)
    within = jnp.cumsum(active, axis=1) - 1
    layer_z = row_ids // YBLOCKS % LZ
    layer_y = row_ids % YBLOCKS % YR
    base_value = (layer_z * YR + layer_y) * CAPL
    table = jnp.where(active > 0, base_value[:, None] + within, -1)
    return table.reshape(ZBLOCKS, YBLOCKS, LX).astype(jnp.int32)


def shard_levels(stream_key, extent, pieces, least, top_value):
    def one(axis_at, shards_of):
        draws = jax.random.uniform(jax.random.fold_in(jax.random.fold_in(stream_key, 6), axis_at), (shards_of,), jnp.float32, least / len(pieces), top_value / len(pieces))
        return jnp.repeat(jnp.exp(draws), extent[axis_at] // shards_of).reshape((-1,) + (1,) * (len(extent) - axis_at - 1))

    level = one(*pieces[0])
    for cut in pieces[1:]:
        level = level * one(*cut)
    return level


def gaussian(rng, shape, width, reach, cuts=(), held_as=jnp.bfloat16):
    array = width * jax.random.normal(rng, shape, jnp.float32)
    if cuts:
        array = array * shard_levels(rng, shape, cuts, -0.22, 0.18)
    return jnp.clip(array, -reach, reach).astype(held_as)


def setup_inputs(seed: int = 0) -> dict:
    key_list = jax.random.split(jax.random.key(seed), 5)
    return {
        "features": gaussian(key_list[0], (BLOCKS, CH, 512), 1.0, 6.0, ((0, 32),)),
        "cotangent": gaussian(key_list[1], (BLOCKS, CH, 512), 1.0, 6.0, ((0, 32),)),
        "weight": gaussian(key_list[2], (CH, 27 * CH), (27 * CH) ** -0.5, 0.15625),
        "block_table": draw_block_table(jax.random.fold_in(key_list[4], 71), 0),
    }


def neighbours(block_table):
    capacity = LZ * YR * CAPL
    row_ids = jnp.arange(BLOCKS).astype(jnp.int32)
    device_ids = row_ids // capacity
    slot_ids = row_ids % capacity
    z_pos = device_ids // N_TILE * LZ + slot_ids // (YR * CAPL)
    y_pos = device_ids % N_TILE * YR + slot_ids // CAPL % YR
    table_rows = block_table[z_pos, y_pos]
    matches = table_rows == slot_ids[:, None]
    positions = jnp.arange(LX).astype(jnp.int32)
    x_pos = lax.optimization_barrier(jnp.sum(jnp.where(matches, positions[None, :], 0), axis=1)).astype(jnp.int32)
    is_valid = jnp.any(matches, axis=1)
    found_lists = []
    for step_z in (-1, 0, 1):
        for step_y in (-1, 0, 1):
            for step_x in (-1, 0, 1):
                near_z = z_pos + step_z
                near_y = y_pos + step_y
                near_x = x_pos + step_x
                inside = (near_z >= 0) & (near_z < ZBLOCKS) & (near_y >= 0) & (near_y < YBLOCKS) & (near_x >= 0) & (near_x < LX)
                clip_z = jnp.clip(near_z, 0, ZBLOCKS - 1).astype(jnp.int32)
                clip_y = jnp.clip(near_y, 0, YBLOCKS - 1).astype(jnp.int32)
                clip_x = jnp.clip(near_x, 0, LX - 1).astype(jnp.int32)
                local_index = block_table[clip_z, clip_y, clip_x]
                owner = clip_z // LZ * N_TILE + clip_y // YR
                found_lists.append(jnp.where(inside & (local_index >= 0), owner * capacity + local_index, -1).astype(jnp.int32))
    return (jnp.stack(found_lists, axis=1), is_valid)

def padded_cube(volume, indices):
    keep_mask = (indices >= 0).astype(volume.dtype)
    gathered = volume[jnp.maximum(indices, 0)] * keep_mask[:, None, None, None, None]
    whole = gathered.reshape(3, 3, 3, CH, 8, 8, 8).transpose(3, 0, 4, 1, 5, 2, 6).reshape(CH, 24, 24, 24)
    return whole[:, 7:17, 7:17, 7:17]

def unfold_cube(cube_data):
    windows = [cube_data[:, from_z:from_z + 8, from_y:from_y + 8, from_x:from_x + 8] for from_z in range(3) for from_y in range(3) for from_x in range(3)]
    return jnp.stack(windows, axis=0).reshape(27 * CH, 512)

def reference(features, cotangent, weight, block_table):
    neighbour_index, is_valid = neighbours(block_table)
    volume_x = features.reshape(BLOCKS, CH, 8, 8, 8)
    volume_g = cotangent.reshape(BLOCKS, CH, 8, 8, 8)
    back_weight = jnp.transpose(weight.reshape(CH, 27, CH)[:, ::-1, :], (2, 1, 0)).reshape(CH, 27 * CH)

    def block_step(grad_weight, inputs):
        indices, valid_here, own_grad = inputs
        cols_x = unfold_cube(padded_cube(volume_x, indices))
        cols_g = unfold_cube(padded_cube(volume_g, indices))
        valid_mask = valid_here.astype(jnp.float32)
        forward_part = jnp.dot(weight, cols_x, preferred_element_type=jnp.float32) * valid_mask
        backward_part = jnp.dot(back_weight, cols_g, preferred_element_type=jnp.float32) * valid_mask
        weight_term = jnp.dot(own_grad, cols_x.T, preferred_element_type=jnp.float32) * valid_mask
        return (grad_weight + weight_term, (forward_part.astype(jnp.bfloat16), backward_part.astype(jnp.bfloat16)))
    summed, outputs = lax.scan(block_step, jnp.zeros((CH, 27 * CH), jnp.float32), (neighbour_index, is_valid, cotangent))
    voxels = jnp.sum((block_table >= 0).astype(jnp.float32)) * 512.0
    return (outputs[0], outputs[1], summed / jnp.sqrt(voxels))
```

```python
import functools

import jax
import jax.numpy as jnp
from jax import lax
from jax.experimental import pallas as pl
from jax.experimental.pallas import tpu as pltpu
from jax.sharding import PartitionSpec as P

LZ = 1
YR = 2
LX = 8
CAPL = 4
CH = 64
SLOTS = LZ * YR * CAPL
PAIRS = 14
MESH = pl.DeviceIdType.MESH
F32 = jnp.float32
BF16 = jnp.bfloat16


def kernel(n_slab, n_tile, rows,
           tab, pos, valid, scale, x_ref, g_ref, w_ref,
           conv_ref, grad_ref, gw_ref,
           t_buf, d_buf, c_buf, acc, zs, zr, ys, yr, es, er,
           pay, rb1, s1, rb2, f1, fb,
           hs_sem, hr_sem, a_s, a_r, b_s, b_r, c_s, c_r, e_s, e_r):
    slab = lax.axis_index("slab")
    tile = lax.axis_index("tile")
    ch1 = rows // n_tile
    ch2 = ch1 // n_slab

    def has(dz, dt):
        ok = None
        for v, d, n in ((slab, dz, n_slab), (tile, dt, n_tile)):
            if d:
                c = (v > 0) if d < 0 else (v < n - 1)
                ok = c if ok is None else jnp.logical_and(ok, c)
        return ok

    barrier = pltpu.get_barrier_semaphore()
    for d in range(1, n_tile):
        pl.semaphore_signal(barrier, inc=1, device_id=(slab, lax.rem(tile + d, n_tile)), device_id_type=MESH)
    for d in range(1, n_slab):
        pl.semaphore_signal(barrier, inc=1, device_id=(lax.rem(slab + d, n_slab), tile), device_id_type=MESH)
    diagonals = [(dz, dt) for dz in (-1, 1) for dt in (-1, 1)]
    for dz, dt in diagonals:
        @pl.when(has(dz, dt))
        def _():
            pl.semaphore_signal(barrier, inc=1, device_id=(slab + dz, tile + dt), device_id_type=MESH)

    def to_rows(s, y_side):
        both = jnp.concatenate([x_ref[s].astype(F32), g_ref[s].astype(F32)], axis=0)
        r = both.T
        r4 = r.reshape(8, 8, 8, 2 * CH)
        t_buf[s] = r4
        zs[0, s] = r[0:64].astype(BF16)
        zs[1, s] = r[448:512].astype(BF16)
        yrow = 0 if y_side == 0 else 7
        q = s - CAPL * y_side
        ys[y_side, q] = r4[:, yrow].reshape(64, 2 * CH).astype(BF16)
        es[0, y_side, q] = r4[0, yrow]
        es[1, y_side, q] = r4[7, yrow]

    def lower(s, _):
        to_rows(s, 0)
        return 0

    def upper(s, _):
        to_rows(s, 1)
        return 0

    lax.fori_loop(0, CAPL, lower, 0)
    lax.fori_loop(CAPL, SLOTS, upper, 0)

    z_near = (slab > 0).astype(jnp.int32) + (slab < n_slab - 1).astype(jnp.int32)
    t_near = (tile > 0).astype(jnp.int32) + (tile < n_tile - 1).astype(jnp.int32)
    pl.semaphore_wait(barrier, n_tile - 1 + n_slab - 1 + z_near * t_near)

    dirs = [(dz, dt) for dz in (-1, 0, 1) for dt in (-1, 0, 1) if dz or dt]
    copies = {}
    for m, (dz, dt) in enumerate(dirs):
        zi, yi = (dz + 1) // 2, (dt + 1) // 2
        if dt == 0:
            src, dst = zs.at[zi], zr.at[1 - zi, pl.ds(0, SLOTS)]
        elif dz == 0:
            src, dst = ys.at[yi], yr.at[1 - yi, pl.ds(0, CAPL)]
        else:
            src, dst = es.at[zi, yi], er.at[1 - zi, 1 - yi, pl.ds(0, CAPL)]
        copies[(dz, dt)] = pltpu.make_async_remote_copy(
            src_ref=src, dst_ref=dst, send_sem=hs_sem.at[m], recv_sem=hr_sem.at[7 - m],
            device_id=(slab + dz, tile + dt), device_id_type=MESH)
    for m in dirs:
        @pl.when(has(*m))
        def _():
            copies[m].start()

    t_buf[SLOTS] = jnp.zeros((8, 8, 8, 2 * CH), F32)
    for side in range(2):
        zr[side, SLOTS] = jnp.zeros((64, 2 * CH), BF16)
        yr[side, CAPL] = jnp.zeros((64, 2 * CH), BF16)
        for other in range(2):
            er[side, other, CAPL] = jnp.zeros((8, 2 * CH), F32)

    def clear(z, _):
        d_buf[0, z] = jnp.zeros((18, 8, 2 * CH), F32)
        d_buf[LX + 1, z] = jnp.zeros((18, 8, 2 * CH), F32)
        return 0

    lax.fori_loop(0, 10, clear, 0)

    def inner(b, _):
        for ly in range(YR):
            i = tab[1, 1 + ly, b]
            d_buf[b + 1, 1:9, 1 + 8 * ly:9 + 8 * ly] = t_buf[i]
        return 0

    lax.fori_loop(0, LX, inner, 0)

    for m in dirs:
        @pl.when(has(*m))
        def _():
            copies[(-m[0], -m[1])].wait_recv()

    def outer(b, _):
        for zi in range(2):
            for ly in range(YR):
                i = tab[2 * zi, 1 + ly, b]
                d_buf[b + 1, 9 * zi, 1 + 8 * ly:9 + 8 * ly] = zr[zi, i].astype(F32).reshape(8, 8, 2 * CH)
            for yi in range(2):
                i = tab[2 * zi, 3 * yi, b]
                d_buf[b + 1, 9 * zi, 17 * yi] = er[zi, yi, i]
        for yi in range(2):
            i = tab[1, 3 * yi, b]
            d_buf[b + 1, 1:9, 17 * yi] = yr[yi, i].astype(F32).reshape(8, 8, 2 * CH)
        return 0

    lax.fori_loop(0, LX, outer, 0)

    acc[...] = jnp.zeros_like(acc)

    def first(s, _):
        b = pos[s]
        y0 = s // CAPL * 8

        def plane(z, _):
            mid = d_buf[b + 1, z, pl.ds(y0, 10)]
            left = d_buf[b, z, pl.ds(y0, 10)]
            right = d_buf[b + 2, z, pl.ds(y0, 10)]
            row = lax.broadcasted_iota(jnp.int32, (10, 8, 2 * CH), 1)
            shifted = (
                pltpu.roll(jnp.where(row == 7, left, mid), 1, 1),
                mid,
                pltpu.roll(jnp.where(row == 0, right, mid), 7, 1),
            )
            for dy in range(3):
                for dx in range(3):
                    j = dy * 3 + dx
                    c_buf[s, pl.ds(pl.multiple_of(z * 64, 64), 64), j * 128:(j + 1) * 128] = (
                        shifted[dx][dy:dy + 8].reshape(64, 2 * CH).astype(BF16))
            return 0

        lax.fori_loop(0, 10, plane, 0)
        g = g_ref[s].astype(F32) * valid[s]
        wide = jnp.concatenate([g, jnp.zeros((CH, 128), F32)], axis=1)
        lhs = jnp.concatenate([wide, pltpu.roll(wide, 64, 1), pltpu.roll(wide, 128, 1)], axis=0).astype(BF16)
        acc[...] += jnp.dot(lhs, c_buf[s], preferred_element_type=F32)
        return 0

    lax.fori_loop(0, SLOTS, first, 0)

    lane = lax.broadcasted_iota(jnp.int32, (CH, 128), 1)

    def term(k):
        dz, j = divmod(k, 9)
        return acc[dz * 64:(dz + 1) * 64, j * 128:(j + 1) * 128]

    for p in range(PAIRS):
        other = pltpu.roll(term(2 * p + 1), 64, 1) if 2 * p + 1 < 27 else jnp.zeros((CH, 128), F32)
        pay[p * 64:(p + 1) * 64] = jnp.where(lane < 64, term(2 * p), other)
    pay[PAIRS * 64:] = jnp.zeros((rows - PAIRS * 64, 128), F32)

    def second(s, _):
        r = jnp.dot(c_buf[s], w_ref[...], preferred_element_type=F32)
        o = (r[0:512, 0:128] + r[64:576, 128:256] + r[128:640, 256:384]) * valid[s]
        ot = o.T
        conv_ref[s] = ot[0:CH].astype(BF16)
        grad_ref[s] = ot[CH:2 * CH].astype(BF16)
        return 0

    step1 = []
    for d in range(1, n_tile):
        peer = lax.rem(tile + d, n_tile)
        step1.append(pltpu.make_async_remote_copy(
            src_ref=pay.at[pl.ds(pl.multiple_of(peer * ch1, 8), ch1)], dst_ref=rb1.at[d],
            send_sem=a_s.at[d], recv_sem=a_r.at[d], device_id=(slab, peer), device_id_type=MESH))
    for c in step1:
        c.start()
    lax.fori_loop(0, 3, second, 0)
    for c in step1:
        c.wait_recv()
    total = pay[pl.ds(pl.multiple_of(tile * ch1, 8), ch1)]
    for d in range(1, n_tile):
        total = total + rb1[d]
    s1[...] = total

    step2 = []
    for d in range(1, n_slab):
        peer = lax.rem(slab + d, n_slab)
        step2.append(pltpu.make_async_remote_copy(
            src_ref=s1.at[pl.ds(pl.multiple_of(peer * ch2, 8), ch2)], dst_ref=rb2.at[d],
            send_sem=b_s.at[d], recv_sem=b_r.at[d], device_id=(peer, tile), device_id_type=MESH))
    for c in step2:
        c.start()
    lax.fori_loop(3, 4, second, 0)
    for c in step2:
        c.wait_recv()
    mine = pl.ds(pl.multiple_of(slab * ch2, 8), ch2)
    total = s1[mine]
    for d in range(1, n_slab):
        total = total + rb2[d]
    f1[mine] = total * scale[0]

    step3 = []
    for d in range(1, n_slab):
        step3.append(pltpu.make_async_remote_copy(
            src_ref=f1.at[mine], dst_ref=f1.at[mine],
            send_sem=c_s.at[d], recv_sem=c_r.at[d],
            device_id=(lax.rem(slab + d, n_slab), tile), device_id_type=MESH))
    for c in step3:
        c.start()
    lax.fori_loop(4, 5, second, 0)
    for c in step3:
        c.wait_recv()

    place = pl.ds(pl.multiple_of(tile * ch1, 8), ch1)
    step4 = []
    for d in range(1, n_tile):
        step4.append(pltpu.make_async_remote_copy(
            src_ref=f1, dst_ref=fb.at[place],
            send_sem=e_s.at[d], recv_sem=e_r.at[d],
            device_id=(slab, lax.rem(tile + d, n_tile)), device_id_type=MESH))
    for c in step4:
        c.start()
    fb[place] = f1[...]
    lax.fori_loop(5, SLOTS, second, 0)
    for c in step4:
        c.wait_recv()
    for p in range(PAIRS - 1):
        gw_ref[:, p * 128:(p + 1) * 128] = fb[p * 64:(p + 1) * 64]
    gw_ref[:, (PAIRS - 1) * 128:] = fb[(PAIRS - 1) * 64:PAIRS * 64, 0:64]

    for c in step1 + step2 + step3 + step4:
        c.wait_send()
    for m in dirs:
        @pl.when(has(*m))
        def _():
            copies[m].wait_send()


def shards(n_slab, n_tile, features, cotangent, weight, block_table):
    slab = lax.axis_index("slab")
    tile = lax.axis_index("tile")
    padded = jnp.pad(block_table, ((1, 1), (1, 1), (0, 0)), constant_values=-1)
    near = lax.dynamic_slice(padded, (slab * LZ, tile * YR, 0), (3, YR + 2, LX))
    lead = jnp.array([CAPL, 0, 0, 0], jnp.int32)[None, :, None]
    none = jnp.array([CAPL, SLOTS, SLOTS, CAPL], jnp.int32)[None, :, None]
    tab = jnp.where(near >= 0, near - lead, none)
    own = near[1, 1:1 + YR]
    slot_ids = jnp.arange(SLOTS, dtype=jnp.int32)
    matches = own.reshape(1, YR * LX) == slot_ids[:, None]
    pos = jnp.sum(jnp.where(matches, jnp.arange(YR * LX, dtype=jnp.int32)[None, :] % LX, 0), axis=1)
    valid = jnp.any(matches, axis=1).astype(F32)
    voxels = jnp.sum((block_table >= 0).astype(F32)) * 512.0
    scale = (1.0 / jnp.sqrt(voxels)).reshape(1)

    fw = weight.reshape(CH, 3, 9, CH).transpose(2, 3, 1, 0)
    bw = weight.reshape(CH, 27, CH)[:, ::-1].reshape(CH, 3, 9, CH).transpose(2, 0, 1, 3)
    zero = jnp.zeros_like(fw)
    big = jnp.concatenate(
        [jnp.concatenate([fw, zero], axis=3), jnp.concatenate([zero, bw], axis=3)], axis=1
    ).reshape(9 * 2 * CH, 3 * 2 * CH)

    unit = 8 * n_slab * n_tile
    rows = -(-PAIRS * 64 // unit) * unit
    ch1 = rows // n_tile
    ch2 = ch1 // n_slab
    vmem = pl.BlockSpec(memory_space=pltpu.VMEM)
    smem = pl.BlockSpec(memory_space=pltpu.SMEM)
    dma = pltpu.SemaphoreType.DMA
    flops = 2 * SLOTS * 640 * 1152 * (384 + 192)
    return pl.pallas_call(
        functools.partial(kernel, n_slab, n_tile, rows),
        out_shape=(
            jax.ShapeDtypeStruct((SLOTS, CH, 512), BF16),
            jax.ShapeDtypeStruct((SLOTS, CH, 512), BF16),
            jax.ShapeDtypeStruct((CH, 27 * CH), F32),
        ),
        in_specs=[smem] * 4 + [vmem] * 3,
        out_specs=(vmem, vmem, vmem),
        scratch_shapes=[
            pltpu.VMEM((SLOTS + 1, 8, 8, 8, 128), F32),
            pltpu.VMEM((LX + 2, 10, 18, 8, 128), F32),
            pltpu.VMEM((SLOTS, 640, 1152), BF16),
            pltpu.VMEM((192, 1152), F32),
            pltpu.VMEM((2, SLOTS, 64, 128), BF16),
            pltpu.VMEM((2, SLOTS + 1, 64, 128), BF16),
            pltpu.VMEM((2, CAPL, 64, 128), BF16),
            pltpu.VMEM((2, CAPL + 1, 64, 128), BF16),
            pltpu.VMEM((2, 2, CAPL, 8, 128), F32),
            pltpu.VMEM((2, 2, CAPL + 1, 8, 128), F32),
            pltpu.VMEM((rows, 128), F32),
            pltpu.VMEM((n_tile, ch1, 128), F32),
            pltpu.VMEM((ch1, 128), F32),
            pltpu.VMEM((n_slab, ch2, 128), F32),
            pltpu.VMEM((ch1, 128), F32),
            pltpu.VMEM((rows, 128), F32),
            dma((8,)), dma((8,)),
            dma((n_tile,)), dma((n_tile,)),
            dma((n_slab,)), dma((n_slab,)),
            dma((n_slab,)), dma((n_slab,)),
            dma((n_tile,)), dma((n_tile,)),
        ],
        compiler_params=pltpu.CompilerParams(
            collective_id=0, has_side_effects=True, vmem_limit_bytes=48 * 1024 * 1024
        ),
        cost_estimate=pl.CostEstimate(flops=flops, bytes_accessed=3 << 20, transcendentals=0),
    )(tab, pos, valid, scale, features, cotangent, big)


def solution(mesh):
    placed = (P(("slab", "tile"), None, None), P(("slab", "tile"), None, None), P(), P())
    return jax.shard_map(
        functools.partial(shards, mesh.shape["slab"], mesh.shape["tile"]),
        mesh=mesh,
        in_specs=placed,
        out_specs=(P(("slab", "tile"), None, None), P(("slab", "tile"), None, None), P()),
        check_vma=False,
    )
```

```python
import functools

import jax
import jax.numpy as jnp
from jax import lax
from jax.experimental import pallas as pl
from jax.experimental.pallas import tpu as pltpu
from jax.sharding import PartitionSpec as P

LZ = 1
YR = 2
LX = 8
CAPL = 4
CH = 64
SLOTS = LZ * YR * CAPL
PAIRS = 14
MESH = pl.DeviceIdType.MESH
F32 = jnp.float32
BF16 = jnp.bfloat16


def kernel(n_slab, n_tile, rows,
           table, x_any, g_any, w_any, table_any,
           conv_ref, grad_ref, gw_ref,
           x_ref, g_ref, w_ref, table_v, in_sem, pos, valid, w_big,
           t_buf, d_buf, c_even, c_odd, acc, zs, zr, ys, yr, es, er,
           pay, rb1, s1, rb2, f1, fb,
           hs_sem, hr_sem, a_s, a_r, b_s, b_r, c_s, c_r, e_s, e_r):
    slab = lax.axis_index("slab")
    tile = lax.axis_index("tile")
    ch1 = rows // n_tile
    ch2 = ch1 // n_slab

    def has(dz, dt):
        ok = None
        for v, d, n in ((slab, dz, n_slab), (tile, dt, n_tile)):
            if d:
                c = (v > 0) if d < 0 else (v < n - 1)
                ok = c if ok is None else jnp.logical_and(ok, c)
        return ok

    loads = [
        pltpu.make_async_copy(src, dst, in_sem.at[i])
        for i, (src, dst) in enumerate(
            ((x_any, x_ref), (g_any, g_ref), (w_any, w_ref), (table_any, table_v)))
    ]
    for c in loads:
        c.start()

    def near(zi, yi, b):
        z = slab + zi - 1
        y = tile * YR + yi - 1
        inside = (z >= 0) & (z < n_slab) & (y >= 0) & (y < n_tile * YR)
        v = table[jnp.clip(z, 0, n_slab - 1), b, jnp.clip(y, 0, n_tile * YR - 1)]
        none = CAPL if yi in (0, YR + 1) else SLOTS
        return jnp.where(inside & (v >= 0), jnp.maximum(v - (CAPL if yi == 0 else 0), 0), none)

    barrier = pltpu.get_barrier_semaphore()
    for d in range(1, n_tile):
        pl.semaphore_signal(barrier, inc=1, device_id=(slab, lax.rem(tile + d, n_tile)), device_id_type=MESH)
    for d in range(1, n_slab):
        pl.semaphore_signal(barrier, inc=1, device_id=(lax.rem(slab + d, n_slab), tile), device_id_type=MESH)
    diagonals = [(dz, dt) for dz in (-1, 1) for dt in (-1, 1)]
    for dz, dt in diagonals:
        @pl.when(has(dz, dt))
        def _():
            pl.semaphore_signal(barrier, inc=1, device_id=(slab + dz, tile + dt), device_id_type=MESH)

    def to_rows(s, y_side):
        both = jnp.concatenate([x_ref[s].astype(F32), g_ref[s].astype(F32)], axis=0)
        r = both.T
        r4 = r.reshape(8, 8, 8, 2 * CH)
        t_buf[s] = r4
        zs[0, s] = r[0:64].astype(BF16)
        zs[1, s] = r[448:512].astype(BF16)
        yrow = 0 if y_side == 0 else 7
        q = s - CAPL * y_side
        ys[y_side, q] = r4[:, yrow].reshape(64, 2 * CH).astype(BF16)
        es[0, y_side, q] = r4[0, yrow]
        es[1, y_side, q] = r4[7, yrow]

    for c in loads[:2]:
        c.wait()
    for s in range(SLOTS):
        to_rows(s, s // CAPL)

    z_near = (slab > 0).astype(jnp.int32) + (slab < n_slab - 1).astype(jnp.int32)
    t_near = (tile > 0).astype(jnp.int32) + (tile < n_tile - 1).astype(jnp.int32)
    pl.semaphore_wait(barrier, n_tile - 1 + n_slab - 1 + z_near * t_near)

    dirs = [(dz, dt) for dz in (-1, 0, 1) for dt in (-1, 0, 1) if dz or dt]
    copies = {}
    for m, (dz, dt) in enumerate(dirs):
        zi, yi = (dz + 1) // 2, (dt + 1) // 2
        if dt == 0:
            src, dst = zs.at[zi], zr.at[1 - zi, pl.ds(0, SLOTS)]
        elif dz == 0:
            src, dst = ys.at[yi], yr.at[1 - yi, pl.ds(0, CAPL)]
        else:
            src, dst = es.at[zi, yi], er.at[1 - zi, 1 - yi, pl.ds(0, CAPL)]
        copies[(dz, dt)] = pltpu.make_async_remote_copy(
            src_ref=src, dst_ref=dst, send_sem=hs_sem.at[m], recv_sem=hr_sem.at[7 - m],
            device_id=(slab + dz, tile + dt), device_id_type=MESH)
    for m in dirs:
        @pl.when(has(*m))
        def _():
            copies[m].start()

    for s in range(SLOTS):
        at, found = jnp.int32(0), jnp.float32(0)
        for b in range(LX):
            hit = table[slab, b, tile * YR + s // CAPL] == s
            at = jnp.where(hit, b, at)
            found = jnp.where(hit, 1.0, found)
        pos[s] = at
        valid[s] = found

    for c in loads[2:]:
        c.wait()
    wide_lane = lax.broadcasted_iota(jnp.int32, (CH, 128), 1)
    for p in range(PAIRS):
        if p < PAIRS - 1:
            pair = w_ref[:, p * 128:(p + 1) * 128].astype(F32)
        else:
            pair = jnp.concatenate(
                [w_ref[:, p * 128:27 * CH].astype(F32), jnp.zeros((CH, 64), F32)], axis=1)
        flipped = jnp.concatenate([pair, jnp.zeros((CH, 128), F32)], axis=0).T
        for k in (2 * p, 2 * p + 1):
            if k >= 27:
                continue
            dz, j = divmod(k, 9)
            w_big[j * 128:j * 128 + 64, dz * 128:(dz + 1) * 128] = (
                flipped[k % 2 * 64:k % 2 * 64 + 64].astype(BF16))
            dz, j = divmod(26 - k, 9)
            half = pair if k % 2 else pltpu.roll(pair, 64, 1)
            w_big[j * 128 + 64:(j + 1) * 128, dz * 128:(dz + 1) * 128] = (
                jnp.where(wide_lane >= 64, half, 0.0).astype(BF16))

    t_buf[SLOTS] = jnp.zeros((8, 8, 8, 2 * CH), F32)
    for side in range(2):
        zr[side, SLOTS] = jnp.zeros((64, 2 * CH), BF16)
        yr[side, CAPL] = jnp.zeros((64, 2 * CH), BF16)
        for other in range(2):
            er[side, other, CAPL] = jnp.zeros((8, 2 * CH), F32)

    def clear(z, _):
        d_buf[0, z] = jnp.zeros((18, 8, 2 * CH), F32)
        d_buf[LX + 1, z] = jnp.zeros((18, 8, 2 * CH), F32)
        return 0

    lax.fori_loop(0, 10, clear, 0)

    def inner(b, _):
        for ly in range(YR):
            i = near(1, 1 + ly, b)
            d_buf[b + 1, 1:9, 1 + 8 * ly:9 + 8 * ly] = t_buf[i]
        return 0

    lax.fori_loop(0, LX, inner, 0)

    for m in dirs:
        @pl.when(has(*m))
        def _():
            copies[(-m[0], -m[1])].wait_recv()

    def outer(b, _):
        for zi in range(2):
            for ly in range(YR):
                i = near(2 * zi, 1 + ly, b)
                d_buf[b + 1, 9 * zi, 1 + 8 * ly:9 + 8 * ly] = zr[zi, i].astype(F32).reshape(8, 8, 2 * CH)
            for yi in range(2):
                i = near(2 * zi, 3 * yi, b)
                d_buf[b + 1, 9 * zi, 17 * yi] = er[zi, yi, i]
        for yi in range(2):
            i = near(1, 3 * yi, b)
            d_buf[b + 1, 1:9, 17 * yi] = yr[yi, i].astype(F32).reshape(8, 8, 2 * CH)
        return 0

    lax.fori_loop(0, LX, outer, 0)

    acc[...] = jnp.zeros_like(acc)

    def build(s, c_ref, q):
        b = pos[s]
        y0 = s // CAPL * 8
        row = lax.broadcasted_iota(jnp.int32, (10, 8, 2 * CH), 1)
        for z in range(10):
            mid = d_buf[b + 1, z, pl.ds(y0, 10)]
            left = d_buf[b, z, pl.ds(y0, 10)]
            right = d_buf[b + 2, z, pl.ds(y0, 10)]
            shifted = (
                pltpu.roll(jnp.where(row == 7, left, mid), 1, 1),
                mid,
                pltpu.roll(jnp.where(row == 0, right, mid), 7, 1),
            )
            for dy in range(3):
                for dx in range(3):
                    j = dy * 3 + dx
                    c_ref[q, z * 64:(z + 1) * 64, j * 128:(j + 1) * 128] = (
                        shifted[dx][dy:dy + 8].reshape(64, 2 * CH).astype(BF16))

    def terms(s, c_ref, q):
        g = g_ref[s].astype(F32) * valid[s]
        wide = jnp.concatenate([g, jnp.zeros((CH, 128), F32)], axis=1)
        lhs = jnp.concatenate([wide, pltpu.roll(wide, 64, 1), pltpu.roll(wide, 128, 1)], axis=0).astype(BF16)
        acc[...] += jnp.dot(lhs, c_ref[q], preferred_element_type=F32)

    build(0, c_even, 0)

    def first(q, _):
        terms(2 * q, c_even, q)
        build(2 * q + 1, c_odd, q)
        terms(2 * q + 1, c_odd, q)
        build(jnp.minimum(2 * q + 2, SLOTS - 1), c_even, q + 1)
        return 0

    lax.fori_loop(0, SLOTS // 2, first, 0)

    lane = lax.broadcasted_iota(jnp.int32, (CH, 128), 1)

    def term(k):
        dz, j = divmod(k, 9)
        return acc[dz * 64:(dz + 1) * 64, j * 128:(j + 1) * 128]

    for p in range(PAIRS):
        other = pltpu.roll(term(2 * p + 1), 64, 1) if 2 * p + 1 < 27 else jnp.zeros((CH, 128), F32)
        pay[p * 64:(p + 1) * 64] = jnp.where(lane < 64, term(2 * p), other)
    pay[PAIRS * 64:] = jnp.zeros((rows - PAIRS * 64, 128), F32)

    def second_of(s, c_ref, q):
        r = jnp.dot(c_ref[q], w_big[...], preferred_element_type=F32)
        o = (r[0:512, 0:128] + r[64:576, 128:256] + r[128:640, 256:384]) * valid[s]
        ot = o.T
        conv_ref[s] = ot[0:CH].astype(BF16)
        grad_ref[s] = ot[CH:2 * CH].astype(BF16)

    def second(q, _):
        second_of(2 * q, c_even, q)
        second_of(2 * q + 1, c_odd, q)
        return 0

    step1 = []
    for d in range(1, n_tile):
        peer = lax.rem(tile + d, n_tile)
        step1.append(pltpu.make_async_remote_copy(
            src_ref=pay.at[pl.ds(pl.multiple_of(peer * ch1, 8), ch1)], dst_ref=rb1.at[d],
            send_sem=a_s.at[d], recv_sem=a_r.at[d], device_id=(slab, peer), device_id_type=MESH))
    for c in step1:
        c.start()
    lax.fori_loop(0, 2, second, 0)
    for c in step1:
        c.wait_recv()
    total = pay[pl.ds(pl.multiple_of(tile * ch1, 8), ch1)]
    for d in range(1, n_tile):
        total = total + rb1[d]
    s1[...] = total

    step2 = []
    for d in range(1, n_slab):
        peer = lax.rem(slab + d, n_slab)
        step2.append(pltpu.make_async_remote_copy(
            src_ref=s1.at[pl.ds(pl.multiple_of(peer * ch2, 8), ch2)], dst_ref=rb2.at[d],
            send_sem=b_s.at[d], recv_sem=b_r.at[d], device_id=(peer, tile), device_id_type=MESH))
    for c in step2:
        c.start()
    second_of(4, c_even, 2)
    for c in step2:
        c.wait_recv()
    mine = pl.ds(pl.multiple_of(slab * ch2, 8), ch2)
    total = s1[mine]
    for d in range(1, n_slab):
        total = total + rb2[d]
    count = jnp.sum((table_v[...] >= 0).astype(F32), axis=0, keepdims=True)
    count = jnp.sum(jnp.sum(count, axis=2, keepdims=True), axis=1, keepdims=True)[0]
    f1[mine] = total / jnp.sqrt(count * 512.0)

    step3 = []
    for d in range(1, n_slab):
        step3.append(pltpu.make_async_remote_copy(
            src_ref=f1.at[mine], dst_ref=f1.at[mine],
            send_sem=c_s.at[d], recv_sem=c_r.at[d],
            device_id=(lax.rem(slab + d, n_slab), tile), device_id_type=MESH))
    for c in step3:
        c.start()
    second_of(5, c_odd, 2)
    for c in step3:
        c.wait_recv()

    place = pl.ds(pl.multiple_of(tile * ch1, 8), ch1)
    step4 = []
    for d in range(1, n_tile):
        step4.append(pltpu.make_async_remote_copy(
            src_ref=f1, dst_ref=fb.at[place],
            send_sem=e_s.at[d], recv_sem=e_r.at[d],
            device_id=(slab, lax.rem(tile + d, n_tile)), device_id_type=MESH))
    for c in step4:
        c.start()
    fb[place] = f1[...]
    lax.fori_loop(3, 4, second, 0)
    for c in step4:
        c.wait_recv()
    for p in range(PAIRS - 1):
        gw_ref[:, p * 128:(p + 1) * 128] = fb[p * 64:(p + 1) * 64]
    gw_ref[:, (PAIRS - 1) * 128:] = fb[(PAIRS - 1) * 64:PAIRS * 64, 0:64]

    for c in step1 + step2 + step3 + step4:
        c.wait_send()
    for m in dirs:
        @pl.when(has(*m))
        def _():
            copies[m].wait_send()


def shards(n_slab, n_tile, features, cotangent, weight, block_table):
    table = jnp.transpose(block_table, (0, 2, 1))
    unit = 8 * n_slab * n_tile
    rows = -(-PAIRS * 64 // unit) * unit
    ch1 = rows // n_tile
    ch2 = ch1 // n_slab
    vmem = pl.BlockSpec(memory_space=pltpu.VMEM)
    smem = pl.BlockSpec(memory_space=pltpu.SMEM)
    dma = pltpu.SemaphoreType.DMA
    flops = 2 * SLOTS * 640 * 1152 * (384 + 192)
    return pl.pallas_call(
        functools.partial(kernel, n_slab, n_tile, rows),
        out_shape=(
            jax.ShapeDtypeStruct((SLOTS, CH, 512), BF16),
            jax.ShapeDtypeStruct((SLOTS, CH, 512), BF16),
            jax.ShapeDtypeStruct((CH, 27 * CH), F32),
        ),
        in_specs=[smem] + [pl.BlockSpec(memory_space=pltpu.HBM)] * 4,
        out_specs=(vmem, vmem, vmem),
        scratch_shapes=[
            pltpu.VMEM((SLOTS, CH, 512), BF16),
            pltpu.VMEM((SLOTS, CH, 512), BF16),
            pltpu.VMEM((CH, 27 * CH), BF16),
            pltpu.VMEM(table.shape, jnp.int32),
            dma((4,)),
            pltpu.SMEM((SLOTS,), jnp.int32),
            pltpu.SMEM((SLOTS,), F32),
            pltpu.VMEM((1152, 384), BF16),
            pltpu.VMEM((SLOTS + 1, 8, 8, 8, 128), F32),
            pltpu.VMEM((LX + 2, 10, 18, 8, 128), F32),
            pltpu.VMEM((SLOTS // 2 + 1, 640, 1152), BF16),
            pltpu.VMEM((SLOTS // 2, 640, 1152), BF16),
            pltpu.VMEM((192, 1152), F32),
            pltpu.VMEM((2, SLOTS, 64, 128), BF16),
            pltpu.VMEM((2, SLOTS + 1, 64, 128), BF16),
            pltpu.VMEM((2, CAPL, 64, 128), BF16),
            pltpu.VMEM((2, CAPL + 1, 64, 128), BF16),
            pltpu.VMEM((2, 2, CAPL, 8, 128), F32),
            pltpu.VMEM((2, 2, CAPL + 1, 8, 128), F32),
            pltpu.VMEM((rows, 128), F32),
            pltpu.VMEM((n_tile, ch1, 128), F32),
            pltpu.VMEM((ch1, 128), F32),
            pltpu.VMEM((n_slab, ch2, 128), F32),
            pltpu.VMEM((ch1, 128), F32),
            pltpu.VMEM((rows, 128), F32),
            dma((8,)), dma((8,)),
            dma((n_tile,)), dma((n_tile,)),
            dma((n_slab,)), dma((n_slab,)),
            dma((n_slab,)), dma((n_slab,)),
            dma((n_tile,)), dma((n_tile,)),
        ],
        compiler_params=pltpu.CompilerParams(
            collective_id=0, has_side_effects=True, vmem_limit_bytes=48 * 1024 * 1024
        ),
        cost_estimate=pl.CostEstimate(flops=flops, bytes_accessed=3 << 20, transcendentals=0),
    )(table, features, cotangent, weight, table)


def solution(mesh):
    placed = (P(("slab", "tile"), None, None), P(("slab", "tile"), None, None), P(), P())
    return jax.shard_map(
        functools.partial(shards, mesh.shape["slab"], mesh.shape["tile"]),
        mesh=mesh,
        in_specs=placed,
        out_specs=(P(("slab", "tile"), None, None), P(("slab", "tile"), None, None), P()),
        check_vma=False,
    )
```

```python
import functools

import jax
import jax.numpy as jnp
from jax import lax
from jax.experimental import pallas as pl
from jax.experimental.pallas import tpu as pltpu
from jax.sharding import PartitionSpec as P

LZ = 1
YR = 2
LX = 8
CAPL = 4
CH = 64
SLOTS = LZ * YR * CAPL
PAIRS = 14
SHIFTS = ((0, 1, 2, 3, 4), (5, 6, 7, 8))


def pairs_of(part):
    ks = sorted(9 * dz + j for dz in range(3) for j in SHIFTS[part])
    evens = [k for k in ks if k % 2 == 0]
    odds = [k for k in ks if k % 2]
    return [(k, odds[i] if i < len(odds) else None) for i, k in enumerate(evens)]


def rows_of(part, n_tile):
    unit = 8 * n_tile
    return -(-len(pairs_of(part)) * 64 // unit) * unit

MESH = pl.DeviceIdType.MESH
F32 = jnp.float32
BF16 = jnp.bfloat16


def kernel(n_slab, n_tile,
           table, x_any, g_any, w_any, table_any,
           conv_ref, grad_ref, gw_ref,
           x_ref, g_ref, w_ref, table_v, in_sem, pos, valid, w_big,
           t_buf, d_buf, c_even, c_odd, acc, zs, zr, ys, yr, es, er,
           pay_a, rb1_a, s1_a, rb2_a, f1_a, fb_a,
           pay_b, rb1_b, s1_b, rb2_b, f1_b, fb_b,
           hs_sem, hr_sem, tile_s, tile_r, slab_s, slab_r):
    slab = lax.axis_index("slab")
    tile = lax.axis_index("tile")
    def has(dz, dt):
        ok = None
        for v, d, n in ((slab, dz, n_slab), (tile, dt, n_tile)):
            if d:
                c = (v > 0) if d < 0 else (v < n - 1)
                ok = c if ok is None else jnp.logical_and(ok, c)
        return ok

    loads = [
        pltpu.make_async_copy(src, dst, in_sem.at[i])
        for i, (src, dst) in enumerate(
            ((x_any, x_ref), (g_any, g_ref), (w_any, w_ref), (table_any, table_v)))
    ]
    for c in loads:
        c.start()

    def near(zi, yi, b):
        z = slab + zi - 1
        y = tile * YR + yi - 1
        inside = (z >= 0) & (z < n_slab) & (y >= 0) & (y < n_tile * YR)
        v = table[jnp.clip(z, 0, n_slab - 1), b, jnp.clip(y, 0, n_tile * YR - 1)]
        none = CAPL if yi in (0, YR + 1) else SLOTS
        return jnp.where(inside & (v >= 0), jnp.maximum(v - (CAPL if yi == 0 else 0), 0), none)

    barrier = pltpu.get_barrier_semaphore()
    for d in range(1, n_tile):
        pl.semaphore_signal(barrier, inc=1, device_id=(slab, lax.rem(tile + d, n_tile)), device_id_type=MESH)
    for d in range(1, n_slab):
        pl.semaphore_signal(barrier, inc=1, device_id=(lax.rem(slab + d, n_slab), tile), device_id_type=MESH)
    diagonals = [(dz, dt) for dz in (-1, 1) for dt in (-1, 1)]
    for dz, dt in diagonals:
        @pl.when(has(dz, dt))
        def _():
            pl.semaphore_signal(barrier, inc=1, device_id=(slab + dz, tile + dt), device_id_type=MESH)

    def to_rows(s, y_side):
        both = jnp.concatenate([x_ref[s].astype(F32), g_ref[s].astype(F32)], axis=0)
        r = both.T
        r4 = r.reshape(8, 8, 8, 2 * CH)
        t_buf[s] = r4
        zs[0, s] = r[0:64].astype(BF16)
        zs[1, s] = r[448:512].astype(BF16)
        yrow = 0 if y_side == 0 else 7
        q = s - CAPL * y_side
        ys[y_side, q] = r4[:, yrow].reshape(64, 2 * CH).astype(BF16)
        es[0, y_side, q] = r4[0, yrow]
        es[1, y_side, q] = r4[7, yrow]

    for c in loads[:2]:
        c.wait()
    for s in range(SLOTS):
        to_rows(s, s // CAPL)

    z_near = (slab > 0).astype(jnp.int32) + (slab < n_slab - 1).astype(jnp.int32)
    t_near = (tile > 0).astype(jnp.int32) + (tile < n_tile - 1).astype(jnp.int32)
    pl.semaphore_wait(barrier, n_tile - 1 + n_slab - 1 + z_near * t_near)

    dirs = [(dz, dt) for dz in (-1, 0, 1) for dt in (-1, 0, 1) if dz or dt]
    copies = {}
    for m, (dz, dt) in enumerate(dirs):
        zi, yi = (dz + 1) // 2, (dt + 1) // 2
        if dt == 0:
            src, dst = zs.at[zi], zr.at[1 - zi, pl.ds(0, SLOTS)]
        elif dz == 0:
            src, dst = ys.at[yi], yr.at[1 - yi, pl.ds(0, CAPL)]
        else:
            src, dst = es.at[zi, yi], er.at[1 - zi, 1 - yi, pl.ds(0, CAPL)]
        copies[(dz, dt)] = pltpu.make_async_remote_copy(
            src_ref=src, dst_ref=dst, send_sem=hs_sem.at[m], recv_sem=hr_sem.at[7 - m],
            device_id=(slab + dz, tile + dt), device_id_type=MESH)
    for m in dirs:
        @pl.when(has(*m))
        def _():
            copies[m].start()

    for s in range(SLOTS):
        at, found = jnp.int32(0), jnp.float32(0)
        for b in range(LX):
            hit = table[slab, b, tile * YR + s // CAPL] == s
            at = jnp.where(hit, b, at)
            found = jnp.where(hit, 1.0, found)
        pos[s] = at
        valid[s] = found

    for c in loads[2:]:
        c.wait()
    wide_lane = lax.broadcasted_iota(jnp.int32, (CH, 128), 1)
    for p in range(PAIRS):
        if p < PAIRS - 1:
            pair = w_ref[:, p * 128:(p + 1) * 128].astype(F32)
        else:
            pair = jnp.concatenate(
                [w_ref[:, p * 128:27 * CH].astype(F32), jnp.zeros((CH, 64), F32)], axis=1)
        flipped = jnp.concatenate([pair, jnp.zeros((CH, 128), F32)], axis=0).T
        for k in (2 * p, 2 * p + 1):
            if k >= 27:
                continue
            dz, j = divmod(k, 9)
            w_big[j * 128:j * 128 + 64, dz * 128:(dz + 1) * 128] = (
                flipped[k % 2 * 64:k % 2 * 64 + 64].astype(BF16))
            dz, j = divmod(26 - k, 9)
            half = pair if k % 2 else pltpu.roll(pair, 64, 1)
            w_big[j * 128 + 64:(j + 1) * 128, dz * 128:(dz + 1) * 128] = (
                jnp.where(wide_lane >= 64, half, 0.0).astype(BF16))

    t_buf[SLOTS] = jnp.zeros((8, 8, 8, 2 * CH), F32)
    for side in range(2):
        zr[side, SLOTS] = jnp.zeros((64, 2 * CH), BF16)
        yr[side, CAPL] = jnp.zeros((64, 2 * CH), BF16)
        for other in range(2):
            er[side, other, CAPL] = jnp.zeros((8, 2 * CH), F32)

    def clear(z, _):
        d_buf[0, z] = jnp.zeros((18, 8, 2 * CH), F32)
        d_buf[LX + 1, z] = jnp.zeros((18, 8, 2 * CH), F32)
        return 0

    lax.fori_loop(0, 10, clear, 0)

    def inner(b, _):
        for ly in range(YR):
            i = near(1, 1 + ly, b)
            d_buf[b + 1, 1:9, 1 + 8 * ly:9 + 8 * ly] = t_buf[i]
        return 0

    lax.fori_loop(0, LX, inner, 0)

    for m in dirs:
        @pl.when(has(*m))
        def _():
            copies[(-m[0], -m[1])].wait_recv()

    def outer(b, _):
        for zi in range(2):
            for ly in range(YR):
                i = near(2 * zi, 1 + ly, b)
                d_buf[b + 1, 9 * zi, 1 + 8 * ly:9 + 8 * ly] = zr[zi, i].astype(F32).reshape(8, 8, 2 * CH)
            for yi in range(2):
                i = near(2 * zi, 3 * yi, b)
                d_buf[b + 1, 9 * zi, 17 * yi] = er[zi, yi, i]
        for yi in range(2):
            i = near(1, 3 * yi, b)
            d_buf[b + 1, 1:9, 17 * yi] = yr[yi, i].astype(F32).reshape(8, 8, 2 * CH)
        return 0

    lax.fori_loop(0, LX, outer, 0)

    acc[...] = jnp.zeros_like(acc)

    def build(s, c_ref, q, part):
        b = pos[s]
        y0 = s // CAPL * 8
        row = lax.broadcasted_iota(jnp.int32, (10, 8, 2 * CH), 1)
        for z in range(10):
            mid = d_buf[b + 1, z, pl.ds(y0, 10)]
            left = d_buf[b, z, pl.ds(y0, 10)]
            right = d_buf[b + 2, z, pl.ds(y0, 10)]
            shifted = (
                pltpu.roll(jnp.where(row == 7, left, mid), 1, 1),
                mid,
                pltpu.roll(jnp.where(row == 0, right, mid), 7, 1),
            )
            for j in SHIFTS[part]:
                dy, dx = divmod(j, 3)
                c_ref[q, z * 64:(z + 1) * 64, j * 128:(j + 1) * 128] = (
                    shifted[dx][dy:dy + 8].reshape(64, 2 * CH).astype(BF16))

    def terms(s, c_ref, q, part):
        g = g_ref[s].astype(F32) * valid[s]
        wide = jnp.concatenate([g, jnp.zeros((CH, 128), F32)], axis=1)
        lhs = jnp.concatenate([wide, pltpu.roll(wide, 64, 1), pltpu.roll(wide, 128, 1)], axis=0).astype(BF16)
        lo, hi = SHIFTS[part][0] * 128, SHIFTS[part][-1] * 128 + 128
        acc[:, lo:hi] += jnp.dot(lhs, c_ref[q, :, lo:hi], preferred_element_type=F32)

    def all_terms(part):
        build(0, c_even, 0, part)

        def step(q, _):
            terms(2 * q, c_even, q, part)
            build(2 * q + 1, c_odd, q, part)
            terms(2 * q + 1, c_odd, q, part)
            build(jnp.minimum(2 * q + 2, SLOTS - 1), c_even, q + 1, part)
            return 0

        lax.fori_loop(0, SLOTS // 2, step, 0)

    def second_of(s, c_ref, q):
        r = jnp.dot(c_ref[q], w_big[...], preferred_element_type=F32)
        o = (r[0:512, 0:128] + r[64:576, 128:256] + r[128:640, 256:384]) * valid[s]
        ot = o.T
        conv_ref[s] = ot[0:CH].astype(BF16)
        grad_ref[s] = ot[CH:2 * CH].astype(BF16)

    lane = lax.broadcasted_iota(jnp.int32, (CH, 128), 1)
    bufs = ((pay_a, rb1_a, s1_a, rb2_a, f1_a, fb_a), (pay_b, rb1_b, s1_b, rb2_b, f1_b, fb_b))

    def term(k):
        dz, j = divmod(k, 9)
        return acc[dz * 64:(dz + 1) * 64, j * 128:(j + 1) * 128]

    def chunk(part):
        return rows_of(part, n_tile) // n_tile

    def own(part):
        return pl.ds(pl.multiple_of(tile * chunk(part), 8), chunk(part))

    def sum_tile_start(part):
        pay, rb1 = bufs[part][:2]
        used = len(pairs_of(part)) * 64
        for p, (ke, ko) in enumerate(pairs_of(part)):
            odd = jnp.zeros((CH, 128), F32) if ko is None else pltpu.roll(term(ko), 64, 1)
            pay[p * 64:(p + 1) * 64] = jnp.where(lane < 64, term(ke), odd)
        if rows_of(part, n_tile) > used:
            pay[used:] = jnp.zeros((rows_of(part, n_tile) - used, 128), F32)
        started = []
        for d in range(1, n_tile):
            peer = lax.rem(tile + d, n_tile)
            started.append(pltpu.make_async_remote_copy(
                src_ref=pay.at[pl.ds(pl.multiple_of(peer * chunk(part), 8), chunk(part))],
                dst_ref=rb1.at[d], send_sem=tile_s.at[2 * part, d], recv_sem=tile_r.at[2 * part, d],
                device_id=(slab, peer), device_id_type=MESH))
        for c in started:
            c.start()
        return started

    def sum_slab_start(part, before):
        pay, rb1, s1, rb2 = bufs[part][:4]
        for c in before:
            c.wait_recv()
        total = pay[own(part)]
        for d in range(1, n_tile):
            total = total + rb1[d]
        s1[...] = total
        rb2[slab] = total
        started = []
        for d in range(1, n_slab):
            started.append(pltpu.make_async_remote_copy(
                src_ref=s1, dst_ref=rb2.at[slab],
                send_sem=slab_s.at[part, d], recv_sem=slab_r.at[part, d],
                device_id=(lax.rem(slab + d, n_slab), tile), device_id_type=MESH))
        for c in started:
            c.start()
        return started

    def spread_start(part, before):
        rb2, f1, fb = bufs[part][3:]
        for c in before:
            c.wait_recv()
        total = rb2[0]
        for z in range(1, n_slab):
            total = total + rb2[z]
        count = jnp.sum((table_v[...] >= 0).astype(F32), axis=0, keepdims=True)
        count = jnp.sum(jnp.sum(count, axis=2, keepdims=True), axis=1, keepdims=True)[0]
        total = total / jnp.sqrt(count * 512.0)
        f1[...] = total
        fb[own(part)] = total
        started = []
        for d in range(1, n_tile):
            started.append(pltpu.make_async_remote_copy(
                src_ref=f1, dst_ref=fb.at[own(part)],
                send_sem=tile_s.at[2 * part + 1, d], recv_sem=tile_r.at[2 * part + 1, d],
                device_id=(slab, lax.rem(tile + d, n_tile)), device_id_type=MESH))
        for c in started:
            c.start()
        return started

    def finish(part, before):
        fb = bufs[part][5]
        for c in before:
            c.wait_recv()
        for p, (ke, ko) in enumerate(pairs_of(part)):
            both = fb[p * 64:(p + 1) * 64]
            gw_ref[:, ke * 64:ke * 64 + 64] = both[:, 0:64]
            if ko is not None:
                gw_ref[:, ko * 64:ko * 64 + 64] = both[:, 64:128]

    all_terms(0)
    a1 = sum_tile_start(0)
    all_terms(1)
    b1 = sum_tile_start(1)
    second_of(0, c_even, 0)
    a2 = sum_slab_start(0, a1)
    second_of(1, c_odd, 0)
    second_of(2, c_even, 1)
    b2 = sum_slab_start(1, b1)
    second_of(3, c_odd, 1)
    a3 = spread_start(0, a2)
    second_of(4, c_even, 2)
    second_of(5, c_odd, 2)
    b3 = spread_start(1, b2)
    second_of(6, c_even, 3)
    second_of(7, c_odd, 3)
    finish(0, a3)
    finish(1, b3)

    for c in a1 + b1 + a2 + b2 + a3 + b3:
        c.wait_send()
    for m in dirs:
        @pl.when(has(*m))
        def _():
            copies[m].wait_send()


def shards(n_slab, n_tile, features, cotangent, weight, block_table):
    table = jnp.transpose(block_table, (0, 2, 1))
    vmem = pl.BlockSpec(memory_space=pltpu.VMEM)
    smem = pl.BlockSpec(memory_space=pltpu.SMEM)
    dma = pltpu.SemaphoreType.DMA
    sums = []
    for part in range(2):
        rows = rows_of(part, n_tile)
        ch = rows // n_tile
        sums += [
            pltpu.VMEM((rows, 128), F32),
            pltpu.VMEM((n_tile, ch, 128), F32),
            pltpu.VMEM((ch, 128), F32),
            pltpu.VMEM((n_slab, ch, 128), F32),
            pltpu.VMEM((ch, 128), F32),
            pltpu.VMEM((rows, 128), F32),
        ]
    flops = 2 * SLOTS * 640 * 1152 * (384 + 192)
    return pl.pallas_call(
        functools.partial(kernel, n_slab, n_tile),
        out_shape=(
            jax.ShapeDtypeStruct((SLOTS, CH, 512), BF16),
            jax.ShapeDtypeStruct((SLOTS, CH, 512), BF16),
            jax.ShapeDtypeStruct((CH, 27 * CH), F32),
        ),
        in_specs=[smem] + [pl.BlockSpec(memory_space=pl.ANY)] * 4,
        out_specs=(vmem, vmem, vmem),
        scratch_shapes=[
            pltpu.VMEM((SLOTS, CH, 512), BF16),
            pltpu.VMEM((SLOTS, CH, 512), BF16),
            pltpu.VMEM((CH, 27 * CH), BF16),
            pltpu.VMEM(table.shape, jnp.int32),
            dma((4,)),
            pltpu.SMEM((SLOTS,), jnp.int32),
            pltpu.SMEM((SLOTS,), F32),
            pltpu.VMEM((1152, 384), BF16),
            pltpu.VMEM((SLOTS + 1, 8, 8, 8, 128), F32),
            pltpu.VMEM((LX + 2, 10, 18, 8, 128), F32),
            pltpu.VMEM((SLOTS // 2 + 1, 640, 1152), BF16),
            pltpu.VMEM((SLOTS // 2, 640, 1152), BF16),
            pltpu.VMEM((192, 1152), F32),
            pltpu.VMEM((2, SLOTS, 64, 128), BF16),
            pltpu.VMEM((2, SLOTS + 1, 64, 128), BF16),
            pltpu.VMEM((2, CAPL, 64, 128), BF16),
            pltpu.VMEM((2, CAPL + 1, 64, 128), BF16),
            pltpu.VMEM((2, 2, CAPL, 8, 128), F32),
            pltpu.VMEM((2, 2, CAPL + 1, 8, 128), F32),
            *sums,
            dma((8,)), dma((8,)),
            dma((4, n_tile)), dma((4, n_tile)),
            dma((2, n_slab)), dma((2, n_slab)),
        ],
        compiler_params=pltpu.CompilerParams(
            collective_id=0, has_side_effects=True, vmem_limit_bytes=60 * 1024 * 1024
        ),
        cost_estimate=pl.CostEstimate(flops=flops, bytes_accessed=3 << 20, transcendentals=0),
    )(table, features, cotangent, weight, table)


def solution(mesh):
    placed = (P(("slab", "tile"), None, None), P(("slab", "tile"), None, None), P(), P())
    return jax.shard_map(
        functools.partial(shards, mesh.shape["slab"], mesh.shape["tile"]),
        mesh=mesh,
        in_specs=placed,
        out_specs=(P(("slab", "tile"), None, None), P(("slab", "tile"), None, None), P()),
        check_vma=False,
    )
```

```python
import functools

import jax
import jax.numpy as jnp
from jax import lax
from jax.experimental import pallas as pl
from jax.experimental.pallas import tpu as pltpu
from jax.sharding import PartitionSpec as P

LZ = 1
YR = 2
LX = 8
CAPL = 4
CH = 64
SLOTS = LZ * YR * CAPL
PAIRS = 14
MESH = pl.DeviceIdType.MESH
F32 = jnp.float32
BF16 = jnp.bfloat16
PAIRED = (((1, 0), (4, 3), (7, 6)), ((2, 5), (8, None)))
ALL_PAIRS = PAIRED[0] + PAIRED[1]
HALF = len(ALL_PAIRS) * 128


def rows_of(part, n_tile):
    unit = 8 * n_tile
    return -(-len(PAIRED[part]) * 192 // unit) * unit


def kernel(n_slab, n_tile,
           table, x_any, g_any, w_any, table_any,
           conv_ref, grad_ref, gw_ref,
           x_ref, g_ref, w_ref, table_v, in_sem, pos, valid, w_x, w_g,
           t_buf, d_buf, c_even, c_odd, f_all, h_all, zs, zr, ys, yr, es, er,
           pay_a, rb1_a, s1_a, rb2_a, f1_a, fb_a,
           pay_b, rb1_b, s1_b, rb2_b, f1_b, fb_b,
           hs_sem, hr_sem, tile_s, tile_r, slab_s, slab_r):
    slab = lax.axis_index("slab")
    tile = lax.axis_index("tile")
    def has(dz, dt):
        ok = None
        for v, d, n in ((slab, dz, n_slab), (tile, dt, n_tile)):
            if d:
                c = (v > 0) if d < 0 else (v < n - 1)
                ok = c if ok is None else jnp.logical_and(ok, c)
        return ok

    loads = [
        pltpu.make_async_copy(src, dst, in_sem.at[i])
        for i, (src, dst) in enumerate(
            ((x_any, x_ref), (g_any, g_ref), (w_any, w_ref), (table_any, table_v)))
    ]
    for c in loads:
        c.start()

    def near(zi, yi, b):
        z = slab + zi - 1
        y = tile * YR + yi - 1
        inside = (z >= 0) & (z < n_slab) & (y >= 0) & (y < n_tile * YR)
        v = table[jnp.clip(z, 0, n_slab - 1), b, jnp.clip(y, 0, n_tile * YR - 1)]
        none = CAPL if yi in (0, YR + 1) else SLOTS
        return jnp.where(inside & (v >= 0), jnp.maximum(v - (CAPL if yi == 0 else 0), 0), none)

    barrier = pltpu.get_barrier_semaphore()
    for d in range(1, n_tile):
        pl.semaphore_signal(barrier, inc=1, device_id=(slab, lax.rem(tile + d, n_tile)), device_id_type=MESH)
    for d in range(1, n_slab):
        pl.semaphore_signal(barrier, inc=1, device_id=(lax.rem(slab + d, n_slab), tile), device_id_type=MESH)
    diagonals = [(dz, dt) for dz in (-1, 1) for dt in (-1, 1)]
    for dz, dt in diagonals:
        @pl.when(has(dz, dt))
        def _():
            pl.semaphore_signal(barrier, inc=1, device_id=(slab + dz, tile + dt), device_id_type=MESH)

    def to_rows(s, y_side):
        both = jnp.concatenate([x_ref[s].astype(F32), g_ref[s].astype(F32)], axis=0)
        r = both.T
        r4 = r.reshape(8, 8, 8, 2 * CH)
        t_buf[s] = r4
        zs[0, s] = r[0:64].astype(BF16)
        zs[1, s] = r[448:512].astype(BF16)
        yrow = 0 if y_side == 0 else 7
        q = s - CAPL * y_side
        ys[y_side, q] = r4[:, yrow].reshape(64, 2 * CH).astype(BF16)
        es[0, y_side, q] = r4[0, yrow]
        es[1, y_side, q] = r4[7, yrow]

    dirs = [(dz, dt) for dz in (-1, 0, 1) for dt in (-1, 0, 1) if dz or dt]
    copies = {}
    for m, (dz, dt) in enumerate(dirs):
        zi, yi = (dz + 1) // 2, (dt + 1) // 2
        if dt == 0:
            spans = [pl.ds(h * CAPL, CAPL) for h in range(YR)]
            refs = [(zs.at[zi, q], zr.at[1 - zi, q]) for q in spans]
        elif dz == 0:
            refs = [(ys.at[yi], yr.at[1 - yi, pl.ds(0, CAPL)])]
        else:
            refs = [(es.at[zi, yi], er.at[1 - zi, 1 - yi, pl.ds(0, CAPL)])]
        copies[(dz, dt)] = [pltpu.make_async_remote_copy(
            src_ref=src, dst_ref=dst, send_sem=hs_sem.at[m, h], recv_sem=hr_sem.at[7 - m, h],
            device_id=(slab + dz, tile + dt), device_id_type=MESH) for h, (src, dst) in enumerate(refs)]

    for c in loads[:2]:
        c.wait()
    for h in range(YR):
        for s in range(h * CAPL, (h + 1) * CAPL):
            to_rows(s, h)
        if h == 0:
            z_near = (slab > 0).astype(jnp.int32) + (slab < n_slab - 1).astype(jnp.int32)
            t_near = (tile > 0).astype(jnp.int32) + (tile < n_tile - 1).astype(jnp.int32)
            pl.semaphore_wait(barrier, n_tile - 1 + n_slab - 1 + z_near * t_near)
        for m in dirs:
            if m[1] in (0, 2 * h - 1):
                @pl.when(has(*m))
                def _():
                    copies[m][h if m[1] == 0 else 0].start()

    for s in range(SLOTS):
        at, found = jnp.int32(0), jnp.float32(0)
        for b in range(LX):
            hit = table[slab, b, tile * YR + s // CAPL] == s
            at = jnp.where(hit, b, at)
            found = jnp.where(hit, 1.0, found)
        pos[s] = at
        valid[s] = found

    for c in loads[2:]:
        c.wait()
    low = lax.broadcasted_iota(jnp.int32, (CH, 128), 1) < 64
    for p in range(PAIRS):
        if p < PAIRS - 1:
            pair = w_ref[:, p * 128:(p + 1) * 128].astype(F32)
        else:
            pair = jnp.concatenate(
                [w_ref[:, p * 128:27 * CH].astype(F32), jnp.zeros((CH, 64), F32)], axis=1)
        f_all[p * 128:(p + 1) * 128] = jnp.concatenate([pair, jnp.zeros((CH, 128), F32)], axis=0).T
        h_all[p * 128:p * 128 + 64] = jnp.where(low, pair, 0.0)
        h_all[p * 128 + 64:(p + 1) * 128] = jnp.where(low, pltpu.roll(pair, 64, 1), 0.0)

    def turned(k):
        return f_all[k * 64:(k + 1) * 64]

    def straight(k):
        return h_all[k * 64:(k + 1) * 64]

    for p, pair in enumerate(ALL_PAIRS):
        for at, j in enumerate(pair):
            x_rows = pl.ds(p * 128 + 64 * at, 64)
            g_rows = pl.ds(p * 128 + 64 * (1 - at), 64)
            if j is None:
                w_x[x_rows] = jnp.zeros((64, 256), BF16)
                w_g[g_rows] = jnp.zeros((64, 256), BF16)
                continue
            w_x[x_rows, 0:128] = jnp.where(low, turned(j), pltpu.roll(turned(9 + j), 64, 1)).astype(BF16)
            w_x[x_rows, 128:256] = turned(18 + j).astype(BF16)
            w_g[g_rows, 0:128] = jnp.where(
                low, straight(17 - j), pltpu.roll(straight(26 - j), 64, 1)).astype(BF16)
            w_g[g_rows, 128:256] = pltpu.roll(straight(8 - j), 64, 1).astype(BF16)

    t_buf[SLOTS] = jnp.zeros((8, 8, 8, 2 * CH), F32)
    for side in range(2):
        zr[side, SLOTS] = jnp.zeros((64, 2 * CH), BF16)
        yr[side, CAPL] = jnp.zeros((64, 2 * CH), BF16)
        for other in range(2):
            er[side, other, CAPL] = jnp.zeros((8, 2 * CH), F32)

    def clear(z, _):
        d_buf[0, z] = jnp.zeros((18, 8, 2 * CH), F32)
        d_buf[LX + 1, z] = jnp.zeros((18, 8, 2 * CH), F32)
        return 0

    lax.fori_loop(0, 10, clear, 0)

    def inner(b, _):
        for ly in range(YR):
            i = near(1, 1 + ly, b)
            d_buf[b + 1, 1:9, 1 + 8 * ly:9 + 8 * ly] = t_buf[i]
        return 0

    lax.fori_loop(0, LX, inner, 0)

    for m in dirs:
        @pl.when(has(*m))
        def _():
            for c in copies[(-m[0], -m[1])]:
                c.wait_recv()

    def outer(b, _):
        for zi in range(2):
            for ly in range(YR):
                i = near(2 * zi, 1 + ly, b)
                d_buf[b + 1, 9 * zi, 1 + 8 * ly:9 + 8 * ly] = zr[zi, i].astype(F32).reshape(8, 8, 2 * CH)
            for yi in range(2):
                i = near(2 * zi, 3 * yi, b)
                d_buf[b + 1, 9 * zi, 17 * yi] = er[zi, yi, i]
        for yi in range(2):
            i = near(1, 3 * yi, b)
            d_buf[b + 1, 1:9, 17 * yi] = yr[yi, i].astype(F32).reshape(8, 8, 2 * CH)
        return 0

    lax.fori_loop(0, LX, outer, 0)

    bufs = ((pay_a, rb1_a, s1_a, rb2_a, f1_a, fb_a), (pay_b, rb1_b, s1_b, rb2_b, f1_b, fb_b))
    pay_a[...] = jnp.zeros_like(pay_a)
    pay_b[...] = jnp.zeros_like(pay_b)

    def build(s, c_ref, q, part):
        b = pos[s]
        y0 = s // CAPL * 8
        row = lax.broadcasted_iota(jnp.int32, (10, 8, 2 * CH), 1)
        lower = lax.broadcasted_iota(jnp.int32, (10, 8, 2 * CH), 2) < CH
        for z in range(10):
            def put(p, x_val, g_val):
                for at, v in ((p * 128, x_val), (HALF + p * 128, g_val)):
                    c_ref[q, z * 64:(z + 1) * 64, at:at + 128] = v.reshape(64, 2 * CH).astype(BF16)

            mid = d_buf[b + 1, z, pl.ds(y0, 10)]
            if part == 0:
                left = d_buf[b, z, pl.ds(y0, 10)]
                side = pltpu.roll(pltpu.roll(jnp.where(row == 7, left, mid), 1, 1), CH, 2)
                x_val = jnp.where(lower, mid, side)
                g_val = jnp.where(lower, side, mid)
                for dy in range(3):
                    put(dy, x_val[dy:dy + 8], g_val[dy:dy + 8])
            else:
                right = d_buf[b + 2, z, pl.ds(y0, 10)]
                one = pltpu.roll(jnp.where(row == 0, right, mid), 7, 1)
                two = pltpu.roll(one, CH, 2)
                put(3, jnp.where(lower[0:8], one[0:8], two[1:9]), jnp.where(lower[0:8], two[1:9], one[0:8]))
                put(4, jnp.where(lower[0:8], one[2:10], 0.0), jnp.where(lower[0:8], 0.0, one[2:10]))

    def terms(s, c_ref, q, part):
        g = g_ref[s].astype(F32) * valid[s]
        wide = jnp.concatenate([g, jnp.zeros((CH, 128), F32)], axis=1)
        lhs = jnp.concatenate([wide, pltpu.roll(wide, 64, 1), pltpu.roll(wide, 128, 1)], axis=0).astype(BF16)
        first, many = len(PAIRED[0]) * part, len(PAIRED[part])
        r = jnp.dot(lhs, c_ref[q, :, first * 128:(first + many) * 128], preferred_element_type=F32)
        for p in range(many):
            bufs[part][0][p * 192:(p + 1) * 192] += r[:, p * 128:(p + 1) * 128]

    def all_terms(part):
        build(0, c_even, 0, part)

        def step(q, _):
            terms(2 * q, c_even, q, part)
            build(2 * q + 1, c_odd, q, part)
            terms(2 * q + 1, c_odd, q, part)
            build(jnp.minimum(2 * q + 2, SLOTS - 1), c_even, q + 1, part)
            return 0

        lax.fori_loop(0, SLOTS // 2, step, 0)

    def second_of(s, c_ref, q):
        rx = jnp.dot(c_ref[q, :, 0:HALF], w_x[...], preferred_element_type=F32)
        rg = jnp.dot(c_ref[q, :, HALF:2 * HALF], w_g[...], preferred_element_type=F32)
        lower = lax.broadcasted_iota(jnp.int32, (512, 128), 1) < CH
        crossed = jnp.where(lower, rg[64:576, 0:128], rx[64:576, 0:128])
        o = jnp.where(lower, rx[0:512, 0:128], rg[0:512, 0:128]) + pltpu.roll(crossed, CH, 1)
        o = (o + (rx[128:640, 128:256] + rg[128:640, 128:256])) * valid[s]
        ot = o.T
        conv_ref[s] = ot[0:CH].astype(BF16)
        grad_ref[s] = ot[CH:2 * CH].astype(BF16)

    def chunk(part):
        return rows_of(part, n_tile) // n_tile

    def own(part):
        return pl.ds(pl.multiple_of(tile * chunk(part), 8), chunk(part))

    def sum_tile_start(part):
        pay, rb1 = bufs[part][:2]
        started = []
        for d in range(1, n_tile):
            peer = lax.rem(tile + d, n_tile)
            started.append(pltpu.make_async_remote_copy(
                src_ref=pay.at[pl.ds(pl.multiple_of(peer * chunk(part), 8), chunk(part))],
                dst_ref=rb1.at[d], send_sem=tile_s.at[2 * part, d], recv_sem=tile_r.at[2 * part, d],
                device_id=(slab, peer), device_id_type=MESH))
        for c in started:
            c.start()
        return started

    def sum_slab_start(part, before):
        pay, rb1, s1, rb2 = bufs[part][:4]
        for c in before:
            c.wait_recv()
        total = pay[own(part)]
        for d in range(1, n_tile):
            total = total + rb1[d]
        s1[...] = total
        rb2[slab] = total
        started = []
        for d in range(1, n_slab):
            started.append(pltpu.make_async_remote_copy(
                src_ref=s1, dst_ref=rb2.at[slab],
                send_sem=slab_s.at[part, d], recv_sem=slab_r.at[part, d],
                device_id=(lax.rem(slab + d, n_slab), tile), device_id_type=MESH))
        for c in started:
            c.start()
        return started

    def spread_start(part, before):
        rb2, f1, fb = bufs[part][3:]
        for c in before:
            c.wait_recv()
        total = rb2[0]
        for z in range(1, n_slab):
            total = total + rb2[z]
        count = jnp.sum((table_v[...] >= 0).astype(F32), axis=0, keepdims=True)
        count = jnp.sum(jnp.sum(count, axis=2, keepdims=True), axis=1, keepdims=True)[0]
        total = total / jnp.sqrt(count * 512.0)
        f1[...] = total
        fb[own(part)] = total
        started = []
        for d in range(1, n_tile):
            started.append(pltpu.make_async_remote_copy(
                src_ref=f1, dst_ref=fb.at[own(part)],
                send_sem=tile_s.at[2 * part + 1, d], recv_sem=tile_r.at[2 * part + 1, d],
                device_id=(slab, lax.rem(tile + d, n_tile)), device_id_type=MESH))
        for c in started:
            c.start()
        return started

    def finish(part, before):
        fb = bufs[part][5]
        for c in before:
            c.wait_recv()
        for p, pair in enumerate(PAIRED[part]):
            for dz in range(3):
                both = fb[p * 192 + dz * 64:p * 192 + dz * 64 + 64]
                for at, j in enumerate(pair):
                    if j is not None:
                        k = 9 * dz + j
                        gw_ref[:, k * 64:k * 64 + 64] = both[:, at * 64:at * 64 + 64]

    all_terms(0)
    a1 = sum_tile_start(0)
    all_terms(1)
    b1 = sum_tile_start(1)
    second_of(0, c_even, 0)
    a2 = sum_slab_start(0, a1)
    second_of(1, c_odd, 0)
    second_of(2, c_even, 1)
    b2 = sum_slab_start(1, b1)
    second_of(3, c_odd, 1)
    a3 = spread_start(0, a2)
    second_of(4, c_even, 2)
    second_of(5, c_odd, 2)
    b3 = spread_start(1, b2)
    second_of(6, c_even, 3)
    second_of(7, c_odd, 3)
    finish(0, a3)
    finish(1, b3)

    for c in a1 + b1 + a2 + b2 + a3 + b3:
        c.wait_send()
    for m in dirs:
        @pl.when(has(*m))
        def _():
            for c in copies[m]:
                c.wait_send()


def shards(n_slab, n_tile, features, cotangent, weight, block_table):
    table = jnp.transpose(block_table, (0, 2, 1))
    vmem = pl.BlockSpec(memory_space=pltpu.VMEM)
    smem = pl.BlockSpec(memory_space=pltpu.SMEM)
    dma = pltpu.SemaphoreType.DMA
    sums = []
    for part in range(2):
        rows = rows_of(part, n_tile)
        ch = rows // n_tile
        sums += [
            pltpu.VMEM((rows, 128), F32),
            pltpu.VMEM((n_tile, ch, 128), F32),
            pltpu.VMEM((ch, 128), F32),
            pltpu.VMEM((n_slab, ch, 128), F32),
            pltpu.VMEM((ch, 128), F32),
            pltpu.VMEM((rows, 128), F32),
        ]
    flops = 2 * SLOTS * 640 * 640 * (512 + 192)
    return pl.pallas_call(
        functools.partial(kernel, n_slab, n_tile),
        out_shape=(
            jax.ShapeDtypeStruct((SLOTS, CH, 512), BF16),
            jax.ShapeDtypeStruct((SLOTS, CH, 512), BF16),
            jax.ShapeDtypeStruct((CH, 27 * CH), F32),
        ),
        in_specs=[smem] + [pl.BlockSpec(memory_space=pl.ANY)] * 4,
        out_specs=(vmem, vmem, vmem),
        scratch_shapes=[
            pltpu.VMEM((SLOTS, CH, 512), BF16),
            pltpu.VMEM((SLOTS, CH, 512), BF16),
            pltpu.VMEM((CH, 27 * CH), BF16),
            pltpu.VMEM(table.shape, jnp.int32),
            dma((4,)),
            pltpu.SMEM((SLOTS,), jnp.int32),
            pltpu.SMEM((SLOTS,), F32),
            pltpu.VMEM((HALF, 256), BF16),
            pltpu.VMEM((HALF, 256), BF16),
            pltpu.VMEM((SLOTS + 1, 8, 8, 8, 128), F32),
            pltpu.VMEM((LX + 2, 10, 18, 8, 128), F32),
            pltpu.VMEM((SLOTS // 2 + 1, 640, 2 * HALF), BF16),
            pltpu.VMEM((SLOTS // 2, 640, 2 * HALF), BF16),
            pltpu.VMEM((PAIRS * 128, 128), F32),
            pltpu.VMEM((PAIRS * 128, 128), F32),
            pltpu.VMEM((2, SLOTS, 64, 128), BF16),
            pltpu.VMEM((2, SLOTS + 1, 64, 128), BF16),
            pltpu.VMEM((2, CAPL, 64, 128), BF16),
            pltpu.VMEM((2, CAPL + 1, 64, 128), BF16),
            pltpu.VMEM((2, 2, CAPL, 8, 128), F32),
            pltpu.VMEM((2, 2, CAPL + 1, 8, 128), F32),
            *sums,
            dma((8, 2)), dma((8, 2)),
            dma((4, n_tile)), dma((4, n_tile)),
            dma((2, n_slab)), dma((2, n_slab)),
        ],
        compiler_params=pltpu.CompilerParams(
            collective_id=0, has_side_effects=True, vmem_limit_bytes=60 * 1024 * 1024
        ),
        cost_estimate=pl.CostEstimate(flops=flops, bytes_accessed=3 << 20, transcendentals=0),
    )(table, features, cotangent, weight, table)


def solution(mesh):
    placed = (P(("slab", "tile"), None, None), P(("slab", "tile"), None, None), P(), P())
    return jax.shard_map(
        functools.partial(shards, mesh.shape["slab"], mesh.shape["tile"]),
        mesh=mesh,
        in_specs=placed,
        out_specs=(P(("slab", "tile"), None, None), P(("slab", "tile"), None, None), P()),
        check_vma=False,
    )
```

```python
import functools

import jax
import jax.numpy as jnp
from jax import lax
from jax.experimental import pallas as pl
from jax.experimental.pallas import tpu as pltpu
from jax.sharding import PartitionSpec as P

LZ = 1
YR = 2
LX = 8
CAPL = 4
CH = 64
SLOTS = LZ * YR * CAPL
PAIRS = 14
SHIFTS = ((0, 1, 2, 3, 4), (5, 6, 7, 8))


def pairs_of(part):
    ks = sorted(9 * dz + j for dz in range(3) for j in SHIFTS[part])
    evens = [k for k in ks if k % 2 == 0]
    odds = [k for k in ks if k % 2]
    return [(k, odds[i] if i < len(odds) else None) for i, k in enumerate(evens)]


def rows_of(part, n_tile):
    unit = 8 * n_tile
    return -(-len(pairs_of(part)) * 64 // unit) * unit

MESH = pl.DeviceIdType.MESH
F32 = jnp.float32
BF16 = jnp.bfloat16


def kernel(n_slab, n_tile,
           table, x_any, g_any, w_any, table_any,
           conv_ref, grad_ref, gw_ref,
           x_ref, g_ref, w_ref, table_v, in_sem, pos, valid, w_big,
           t_buf, d_buf, c_even, c_odd, acc, zs, zr, ys, yr, es, er,
           pay_a, rb0_a, hs_a, rb1_a, s1_a, rb2_a, fb_a,
           pay_b, rb0_b, hs_b, rb1_b, s1_b, rb2_b, fb_b,
           hs_sem, hr_sem, pair_s, pair_r, tile_s, tile_r, slab_s, slab_r, hand_s, hand_r):
    slab = lax.axis_index("slab")
    tile = lax.axis_index("tile")
    def has(dz, dt):
        ok = None
        for v, d, n in ((slab, dz, n_slab), (tile, dt, n_tile)):
            if d:
                c = (v > 0) if d < 0 else (v < n - 1)
                ok = c if ok is None else jnp.logical_and(ok, c)
        return ok

    loads = [
        pltpu.make_async_copy(src, dst, in_sem.at[i])
        for i, (src, dst) in enumerate(
            ((x_any, x_ref), (g_any, g_ref), (w_any, w_ref), (table_any, table_v)))
    ]
    for c in loads:
        c.start()

    def near(zi, yi, b):
        z = slab + zi - 1
        y = tile * YR + yi - 1
        inside = (z >= 0) & (z < n_slab) & (y >= 0) & (y < n_tile * YR)
        v = table[jnp.clip(z, 0, n_slab - 1), b, jnp.clip(y, 0, n_tile * YR - 1)]
        none = CAPL if yi in (0, YR + 1) else SLOTS
        return jnp.where(inside & (v >= 0), jnp.maximum(v - (CAPL if yi == 0 else 0), 0), none)

    barrier = pltpu.get_barrier_semaphore()
    for d in range(1, n_tile):
        pl.semaphore_signal(barrier, inc=1, device_id=(slab, lax.rem(tile + d, n_tile)), device_id_type=MESH)
    for d in range(1, n_slab):
        pl.semaphore_signal(barrier, inc=1, device_id=(lax.rem(slab + d, n_slab), tile), device_id_type=MESH)
    diagonals = [(dz, dt) for dz in (-1, 1) for dt in (-1, 1)]
    for dz, dt in diagonals:
        @pl.when(has(dz, dt))
        def _():
            pl.semaphore_signal(barrier, inc=1, device_id=(slab + dz, tile + dt), device_id_type=MESH)

    def to_rows(s, y_side):
        both = jnp.concatenate([x_ref[s].astype(F32), g_ref[s].astype(F32)], axis=0)
        r = both.T
        r4 = r.reshape(8, 8, 8, 2 * CH)
        t_buf[s] = r4
        zs[0, s] = r[0:64].astype(BF16)
        zs[1, s] = r[448:512].astype(BF16)
        yrow = 0 if y_side == 0 else 7
        q = s - CAPL * y_side
        ys[y_side, q] = r4[:, yrow].reshape(64, 2 * CH).astype(BF16)
        es[0, y_side, q] = r4[0, yrow]
        es[1, y_side, q] = r4[7, yrow]

    for c in loads[:2]:
        c.wait()
    for s in range(SLOTS):
        to_rows(s, s // CAPL)

    z_near = (slab > 0).astype(jnp.int32) + (slab < n_slab - 1).astype(jnp.int32)
    t_near = (tile > 0).astype(jnp.int32) + (tile < n_tile - 1).astype(jnp.int32)
    pl.semaphore_wait(barrier, n_tile - 1 + n_slab - 1 + z_near * t_near)

    dirs = [(dz, dt) for dz in (-1, 0, 1) for dt in (-1, 0, 1) if dz or dt]
    copies = {}
    for m, (dz, dt) in enumerate(dirs):
        zi, yi = (dz + 1) // 2, (dt + 1) // 2
        if dt == 0:
            src, dst = zs.at[zi], zr.at[1 - zi, pl.ds(0, SLOTS)]
        elif dz == 0:
            src, dst = ys.at[yi], yr.at[1 - yi, pl.ds(0, CAPL)]
        else:
            src, dst = es.at[zi, yi], er.at[1 - zi, 1 - yi, pl.ds(0, CAPL)]
        copies[(dz, dt)] = pltpu.make_async_remote_copy(
            src_ref=src, dst_ref=dst, send_sem=hs_sem.at[m], recv_sem=hr_sem.at[7 - m],
            device_id=(slab + dz, tile + dt), device_id_type=MESH)
    for m in dirs:
        @pl.when(has(*m))
        def _():
            copies[m].start()

    for s in range(SLOTS):
        at, found = jnp.int32(0), jnp.float32(0)
        for b in range(LX):
            hit = table[slab, b, tile * YR + s // CAPL] == s
            at = jnp.where(hit, b, at)
            found = jnp.where(hit, 1.0, found)
        pos[s] = at
        valid[s] = found

    for c in loads[2:]:
        c.wait()
    wide_lane = lax.broadcasted_iota(jnp.int32, (CH, 128), 1)
    for p in range(PAIRS):
        if p < PAIRS - 1:
            pair = w_ref[:, p * 128:(p + 1) * 128].astype(F32)
        else:
            pair = jnp.concatenate(
                [w_ref[:, p * 128:27 * CH].astype(F32), jnp.zeros((CH, 64), F32)], axis=1)
        flipped = jnp.concatenate([pair, jnp.zeros((CH, 128), F32)], axis=0).T
        for k in (2 * p, 2 * p + 1):
            if k >= 27:
                continue
            dz, j = divmod(k, 9)
            w_big[j * 128:j * 128 + 64, dz * 128:(dz + 1) * 128] = (
                flipped[k % 2 * 64:k % 2 * 64 + 64].astype(BF16))
            dz, j = divmod(26 - k, 9)
            half = pair if k % 2 else pltpu.roll(pair, 64, 1)
            w_big[j * 128 + 64:(j + 1) * 128, dz * 128:(dz + 1) * 128] = (
                jnp.where(wide_lane >= 64, half, 0.0).astype(BF16))

    t_buf[SLOTS] = jnp.zeros((8, 8, 8, 2 * CH), F32)
    for side in range(2):
        zr[side, SLOTS] = jnp.zeros((64, 2 * CH), BF16)
        yr[side, CAPL] = jnp.zeros((64, 2 * CH), BF16)
        for other in range(2):
            er[side, other, CAPL] = jnp.zeros((8, 2 * CH), F32)

    def clear(z, _):
        d_buf[0, z] = jnp.zeros((18, 8, 2 * CH), F32)
        d_buf[LX + 1, z] = jnp.zeros((18, 8, 2 * CH), F32)
        return 0

    lax.fori_loop(0, 10, clear, 0)

    def inner(b, _):
        for ly in range(YR):
            i = near(1, 1 + ly, b)
            d_buf[b + 1, 1:9, 1 + 8 * ly:9 + 8 * ly] = t_buf[i]
        return 0

    lax.fori_loop(0, LX, inner, 0)

    for m in dirs:
        @pl.when(has(*m))
        def _():
            copies[(-m[0], -m[1])].wait_recv()

    def outer(b, _):
        for zi in range(2):
            for ly in range(YR):
                i = near(2 * zi, 1 + ly, b)
                d_buf[b + 1, 9 * zi, 1 + 8 * ly:9 + 8 * ly] = zr[zi, i].astype(F32).reshape(8, 8, 2 * CH)
            for yi in range(2):
                i = near(2 * zi, 3 * yi, b)
                d_buf[b + 1, 9 * zi, 17 * yi] = er[zi, yi, i]
        for yi in range(2):
            i = near(1, 3 * yi, b)
            d_buf[b + 1, 1:9, 17 * yi] = yr[yi, i].astype(F32).reshape(8, 8, 2 * CH)
        return 0

    lax.fori_loop(0, LX, outer, 0)

    acc[...] = jnp.zeros_like(acc)

    def build(s, c_ref, q, part):
        b = pos[s]
        y0 = s // CAPL * 8
        row = lax.broadcasted_iota(jnp.int32, (10, 8, 2 * CH), 1)
        for z in range(10):
            mid = d_buf[b + 1, z, pl.ds(y0, 10)]
            left = d_buf[b, z, pl.ds(y0, 10)]
            right = d_buf[b + 2, z, pl.ds(y0, 10)]
            shifted = (
                pltpu.roll(jnp.where(row == 7, left, mid), 1, 1),
                mid,
                pltpu.roll(jnp.where(row == 0, right, mid), 7, 1),
            )
            for j in SHIFTS[part]:
                dy, dx = divmod(j, 3)
                c_ref[q, z * 64:(z + 1) * 64, j * 128:(j + 1) * 128] = (
                    shifted[dx][dy:dy + 8].reshape(64, 2 * CH).astype(BF16))

    def terms(s, c_ref, q, part):
        g = g_ref[s].astype(F32) * valid[s]
        wide = jnp.concatenate([g, jnp.zeros((CH, 128), F32)], axis=1)
        lhs = jnp.concatenate([wide, pltpu.roll(wide, 64, 1), pltpu.roll(wide, 128, 1)], axis=0).astype(BF16)
        lo, hi = SHIFTS[part][0] * 128, SHIFTS[part][-1] * 128 + 128
        acc[:, lo:hi] += jnp.dot(lhs, c_ref[q, :, lo:hi], preferred_element_type=F32)

    def all_terms(part, start, stop):
        if start == 0:
            build(0, c_even, 0, part)

        def step(q, _):
            terms(2 * q, c_even, q, part)
            build(2 * q + 1, c_odd, q, part)
            terms(2 * q + 1, c_odd, q, part)
            build(jnp.minimum(2 * q + 2, SLOTS - 1), c_even, q + 1, part)
            return 0

        lax.fori_loop(start, stop, step, 0)

    def second_of(s, c_ref, q):
        r = jnp.dot(c_ref[q], w_big[...], preferred_element_type=F32)
        o = (r[0:512, 0:128] + r[64:576, 128:256] + r[128:640, 256:384]) * valid[s]
        ot = o.T
        conv_ref[s] = ot[0:CH].astype(BF16)
        grad_ref[s] = ot[CH:2 * CH].astype(BF16)

    lane = lax.broadcasted_iota(jnp.int32, (CH, 128), 1)
    bufs = ((pay_a, rb0_a, hs_a, rb1_a, s1_a, rb2_a, fb_a), (pay_b, rb0_b, hs_b, rb1_b, s1_b, rb2_b, fb_b))
    chips = n_tile // 2
    core = lax.rem(tile, 2)
    chip = tile // 2
    partner = tile + 1 - 2 * core

    def term(k):
        dz, j = divmod(k, 9)
        return acc[dz * 64:(dz + 1) * 64, j * 128:(j + 1) * 128]

    def chunk(part):
        return rows_of(part, n_tile) // n_tile

    def place(part, which_core, which_chip):
        at = (which_core * chips + which_chip) * chunk(part)
        return pl.ds(pl.multiple_of(at, 8), chunk(part))

    def half(part, which_core):
        size = chips * chunk(part)
        return pl.ds(pl.multiple_of(which_core * size, 8), size)

    def sum_pair_start(part):
        pay, rb0 = bufs[part][:2]
        used = len(pairs_of(part)) * 64
        for p, (ke, ko) in enumerate(pairs_of(part)):
            odd = jnp.zeros((CH, 128), F32) if ko is None else pltpu.roll(term(ko), 64, 1)
            pay[p * 64:(p + 1) * 64] = jnp.where(lane < 64, term(ke), odd)
        if rows_of(part, n_tile) > used:
            pay[used:] = jnp.zeros((rows_of(part, n_tile) - used, 128), F32)
        c = pltpu.make_async_remote_copy(
            src_ref=pay.at[half(part, 1 - core)], dst_ref=rb0,
            send_sem=pair_s.at[part], recv_sem=pair_r.at[part],
            device_id=(slab, partner), device_id_type=MESH)
        c.start()
        return [c]

    def sum_tile_start(part, before):
        pay, rb0, hs, rb1 = bufs[part][:4]
        for c in before:
            c.wait_recv()
        hs[...] = pay[half(part, core)] + rb0[...]
        started = []
        for d in range(1, chips):
            peer = lax.rem(chip + d, chips)
            started.append(pltpu.make_async_remote_copy(
                src_ref=hs.at[place(part, 0, peer)], dst_ref=rb1.at[d],
                send_sem=tile_s.at[2 * part, d], recv_sem=tile_r.at[2 * part, d],
                device_id=(slab, 2 * peer + core), device_id_type=MESH))
        for c in started:
            c.start()
        return started

    def sum_slab_start(part, before):
        hs, rb1, s1, rb2 = bufs[part][2:6]
        for c in before:
            c.wait_recv()
        total = hs[place(part, 0, chip)]
        for d in range(1, chips):
            total = total + rb1[d]
        s1[...] = total
        rb2[slab] = total
        started = []
        for d in range(1, n_slab):
            started.append(pltpu.make_async_remote_copy(
                src_ref=s1, dst_ref=rb2.at[slab],
                send_sem=slab_s.at[part, d], recv_sem=slab_r.at[part, d],
                device_id=(lax.rem(slab + d, n_slab), tile), device_id_type=MESH))
        for c in started:
            c.start()
        return started

    def hand(part, d):
        fb = bufs[part][6]
        at = place(part, core, lax.rem(chip + chips - d, chips))
        c = pltpu.make_async_remote_copy(
            src_ref=fb.at[at], dst_ref=fb.at[at],
            send_sem=hand_s.at[part, d], recv_sem=hand_r.at[part, d],
            device_id=(slab, partner), device_id_type=MESH)
        c.start()
        return c

    def spread_start(part, before):
        rb2, fb = bufs[part][5:]
        for c in before:
            c.wait_recv()
        total = rb2[0]
        for z in range(1, n_slab):
            total = total + rb2[z]
        count = jnp.sum((table_v[...] >= 0).astype(F32), axis=0, keepdims=True)
        count = jnp.sum(jnp.sum(count, axis=2, keepdims=True), axis=1, keepdims=True)[0]
        mine = place(part, core, chip)
        fb[mine] = total / jnp.sqrt(count * 512.0)
        started = []
        for d in range(1, chips):
            peer = lax.rem(chip + d, chips)
            started.append(pltpu.make_async_remote_copy(
                src_ref=fb.at[mine], dst_ref=fb.at[mine],
                send_sem=tile_s.at[2 * part + 1, d], recv_sem=tile_r.at[2 * part + 1, d],
                device_id=(slab, 2 * peer + core), device_id_type=MESH))
        for c in started:
            c.start()
        return started, hand(part, 0)

    def hand_on(part, before):
        started = []
        for d, c in enumerate(before, 1):
            c.wait_recv()
            started.append(hand(part, d))
        return started

    def finish(part, before):
        fb = bufs[part][6]
        for c in before:
            c.wait_recv()
        for p, (ke, ko) in enumerate(pairs_of(part)):
            both = fb[p * 64:(p + 1) * 64]
            gw_ref[:, ke * 64:ke * 64 + 64] = both[:, 0:64]
            if ko is not None:
                gw_ref[:, ko * 64:ko * 64 + 64] = both[:, 64:128]

    all_terms(0, 0, SLOTS // 2)
    a0 = sum_pair_start(0)
    all_terms(1, 0, SLOTS // 4)
    a1 = sum_tile_start(0, a0)
    all_terms(1, SLOTS // 4, SLOTS // 2)
    b0 = sum_pair_start(1)
    second_of(0, c_even, 0)
    b1 = sum_tile_start(1, b0)
    a2 = sum_slab_start(0, a1)
    second_of(1, c_odd, 0)
    second_of(2, c_even, 1)
    b2 = sum_slab_start(1, b1)
    second_of(3, c_odd, 1)
    a3, a4 = spread_start(0, a2)
    second_of(4, c_even, 2)
    a5 = hand_on(0, a3)
    second_of(5, c_odd, 2)
    b3, b4 = spread_start(1, b2)
    second_of(6, c_even, 3)
    second_of(7, c_odd, 3)
    b5 = hand_on(1, b3)
    finish(0, [a4] + a5)
    finish(1, [b4] + b5)

    for c in a0 + a1 + a2 + a3 + [a4] + a5 + b0 + b1 + b2 + b3 + [b4] + b5:
        c.wait_send()
    for m in dirs:
        @pl.when(has(*m))
        def _():
            copies[m].wait_send()


def shards(n_slab, n_tile, features, cotangent, weight, block_table):
    table = jnp.transpose(block_table, (0, 2, 1))
    vmem = pl.BlockSpec(memory_space=pltpu.VMEM)
    smem = pl.BlockSpec(memory_space=pltpu.SMEM)
    dma = pltpu.SemaphoreType.DMA
    sums = []
    for part in range(2):
        rows = rows_of(part, n_tile)
        ch = rows // n_tile
        sums += [
            pltpu.VMEM((rows, 128), F32),
            pltpu.VMEM((rows // 2, 128), F32),
            pltpu.VMEM((rows // 2, 128), F32),
            pltpu.VMEM((n_tile // 2, ch, 128), F32),
            pltpu.VMEM((ch, 128), F32),
            pltpu.VMEM((n_slab, ch, 128), F32),
            pltpu.VMEM((rows, 128), F32),
        ]
    flops = 2 * SLOTS * 640 * 1152 * (384 + 192)
    return pl.pallas_call(
        functools.partial(kernel, n_slab, n_tile),
        out_shape=(
            jax.ShapeDtypeStruct((SLOTS, CH, 512), BF16),
            jax.ShapeDtypeStruct((SLOTS, CH, 512), BF16),
            jax.ShapeDtypeStruct((CH, 27 * CH), F32),
        ),
        in_specs=[smem] + [pl.BlockSpec(memory_space=pl.ANY)] * 4,
        out_specs=(vmem, vmem, vmem),
        scratch_shapes=[
            pltpu.VMEM((SLOTS, CH, 512), BF16),
            pltpu.VMEM((SLOTS, CH, 512), BF16),
            pltpu.VMEM((CH, 27 * CH), BF16),
            pltpu.VMEM(table.shape, jnp.int32),
            dma((4,)),
            pltpu.SMEM((SLOTS,), jnp.int32),
            pltpu.SMEM((SLOTS,), F32),
            pltpu.VMEM((1152, 384), BF16),
            pltpu.VMEM((SLOTS + 1, 8, 8, 8, 128), F32),
            pltpu.VMEM((LX + 2, 10, 18, 8, 128), F32),
            pltpu.VMEM((SLOTS // 2 + 1, 640, 1152), BF16),
            pltpu.VMEM((SLOTS // 2, 640, 1152), BF16),
            pltpu.VMEM((192, 1152), F32),
            pltpu.VMEM((2, SLOTS, 64, 128), BF16),
            pltpu.VMEM((2, SLOTS + 1, 64, 128), BF16),
            pltpu.VMEM((2, CAPL, 64, 128), BF16),
            pltpu.VMEM((2, CAPL + 1, 64, 128), BF16),
            pltpu.VMEM((2, 2, CAPL, 8, 128), F32),
            pltpu.VMEM((2, 2, CAPL + 1, 8, 128), F32),
            *sums,
            dma((8,)), dma((8,)),
            dma((2,)), dma((2,)),
            dma((4, n_tile // 2)), dma((4, n_tile // 2)),
            dma((2, n_slab)), dma((2, n_slab)),
            dma((2, n_tile // 2)), dma((2, n_tile // 2)),
        ],
        compiler_params=pltpu.CompilerParams(
            collective_id=0, has_side_effects=True, vmem_limit_bytes=60 * 1024 * 1024
        ),
        cost_estimate=pl.CostEstimate(flops=flops, bytes_accessed=3 << 20, transcendentals=0),
    )(table, features, cotangent, weight, table)


def solution(mesh):
    placed = (P(("slab", "tile"), None, None), P(("slab", "tile"), None, None), P(), P())
    return jax.shard_map(
        functools.partial(shards, mesh.shape["slab"], mesh.shape["tile"]),
        mesh=mesh,
        in_specs=placed,
        out_specs=(P(("slab", "tile"), None, None), P(("slab", "tile"), None, None), P()),
        check_vma=False,
    )
```

```python
import functools

import jax
import jax.numpy as jnp
from jax import lax
from jax.experimental import pallas as pl
from jax.experimental.pallas import tpu as pltpu
from jax.sharding import PartitionSpec as P

LZ = 1
YR = 2
LX = 8
CAPL = 4
CH = 64
SLOTS = LZ * YR * CAPL
PAIRS = 14
SHIFTS = ((0, 1, 2, 3, 4), (5, 6, 7, 8))


def pairs_of(part):
    ks = sorted(9 * dz + j for dz in range(3) for j in SHIFTS[part])
    evens = [k for k in ks if k % 2 == 0]
    odds = [k for k in ks if k % 2]
    return [(k, odds[i] if i < len(odds) else None) for i, k in enumerate(evens)]


def rows_of(part, n_tile):
    unit = 8 * n_tile
    return -(-len(pairs_of(part)) * 64 // unit) * unit

MESH = pl.DeviceIdType.MESH
F32 = jnp.float32
BF16 = jnp.bfloat16


def kernel(n_slab, n_tile,
           table, x_any, g_any, w_any, table_any,
           conv_ref, grad_ref, gw_ref,
           x_ref, g_ref, w_ref, table_v, in_sem, pos, valid, w_big,
           t_buf, d_buf, c_even, c_odd, acc, zs, zr, ys, yr, es, er,
           pay_a, rb1_a, s1_a, rb2_a, f1_a, fb_a,
           pay_b, rb1_b, s1_b, rb2_b, f1_b, fb_b,
           hs_sem, hr_sem, tile_s, tile_r, slab_s, slab_r):
    slab = lax.axis_index("slab")
    tile = lax.axis_index("tile")
    def has(dz, dt):
        ok = None
        for v, d, n in ((slab, dz, n_slab), (tile, dt, n_tile)):
            if d:
                c = (v > 0) if d < 0 else (v < n - 1)
                ok = c if ok is None else jnp.logical_and(ok, c)
        return ok

    loads = [
        pltpu.make_async_copy(src, dst, in_sem.at[i])
        for i, (src, dst) in enumerate(
            ((x_any, x_ref), (g_any, g_ref), (w_any, w_ref), (table_any, table_v)))
    ]
    for c in loads:
        c.start()

    def near(zi, yi, b):
        z = slab + zi - 1
        y = tile * YR + yi - 1
        inside = (z >= 0) & (z < n_slab) & (y >= 0) & (y < n_tile * YR)
        v = table[jnp.clip(z, 0, n_slab - 1), b, jnp.clip(y, 0, n_tile * YR - 1)]
        none = CAPL if yi in (0, YR + 1) else SLOTS
        return jnp.where(inside & (v >= 0), jnp.maximum(v - (CAPL if yi == 0 else 0), 0), none)

    barrier = pltpu.get_barrier_semaphore()
    for d in range(1, n_tile):
        pl.semaphore_signal(barrier, inc=1, device_id=(slab, lax.rem(tile + d, n_tile)), device_id_type=MESH)
    for d in range(1, n_slab):
        pl.semaphore_signal(barrier, inc=1, device_id=(lax.rem(slab + d, n_slab), tile), device_id_type=MESH)
    diagonals = [(dz, dt) for dz in (-1, 1) for dt in (-1, 1)]
    for dz, dt in diagonals:
        @pl.when(has(dz, dt))
        def _():
            pl.semaphore_signal(barrier, inc=1, device_id=(slab + dz, tile + dt), device_id_type=MESH)

    def to_rows(s, y_side):
        both = jnp.concatenate([x_ref[s].astype(F32), g_ref[s].astype(F32)], axis=0)
        r = both.T
        r4 = r.reshape(8, 8, 8, 2 * CH)
        t_buf[s] = r4
        zs[0, s] = r[0:64].astype(BF16)
        zs[1, s] = r[448:512].astype(BF16)
        yrow = 0 if y_side == 0 else 7
        q = s - CAPL * y_side
        ys[y_side, q] = r4[:, yrow].reshape(64, 2 * CH).astype(BF16)
        es[0, y_side, q] = r4[0, yrow]
        es[1, y_side, q] = r4[7, yrow]

    for c in loads[:2]:
        c.wait()
    for s in range(SLOTS):
        to_rows(s, s // CAPL)

    z_near = (slab > 0).astype(jnp.int32) + (slab < n_slab - 1).astype(jnp.int32)
    t_near = (tile > 0).astype(jnp.int32) + (tile < n_tile - 1).astype(jnp.int32)
    pl.semaphore_wait(barrier, n_tile - 1 + n_slab - 1 + z_near * t_near)

    dirs = [(dz, dt) for dz in (-1, 0, 1) for dt in (-1, 0, 1) if dz or dt]
    copies = {}
    for m, (dz, dt) in enumerate(dirs):
        zi, yi = (dz + 1) // 2, (dt + 1) // 2
        if dt == 0:
            src, dst = zs.at[zi], zr.at[1 - zi, pl.ds(0, SLOTS)]
        elif dz == 0:
            src, dst = ys.at[yi], yr.at[1 - yi, pl.ds(0, CAPL)]
        else:
            src, dst = es.at[zi, yi], er.at[1 - zi, 1 - yi, pl.ds(0, CAPL)]
        copies[(dz, dt)] = pltpu.make_async_remote_copy(
            src_ref=src, dst_ref=dst, send_sem=hs_sem.at[m], recv_sem=hr_sem.at[7 - m],
            device_id=(slab + dz, tile + dt), device_id_type=MESH)
    for m in dirs:
        @pl.when(has(*m))
        def _():
            copies[m].start()

    for s in range(SLOTS):
        at, found = jnp.int32(0), jnp.float32(0)
        for b in range(LX):
            hit = table[slab, b, tile * YR + s // CAPL] == s
            at = jnp.where(hit, b, at)
            found = jnp.where(hit, 1.0, found)
        pos[s] = at
        valid[s] = found

    for c in loads[2:]:
        c.wait()
    wide_lane = lax.broadcasted_iota(jnp.int32, (CH, 128), 1)
    for p in range(PAIRS):
        if p < PAIRS - 1:
            pair = w_ref[:, p * 128:(p + 1) * 128].astype(F32)
        else:
            pair = jnp.concatenate(
                [w_ref[:, p * 128:27 * CH].astype(F32), jnp.zeros((CH, 64), F32)], axis=1)
        flipped = jnp.concatenate([pair, jnp.zeros((CH, 128), F32)], axis=0).T
        for k in (2 * p, 2 * p + 1):
            if k >= 27:
                continue
            dz, j = divmod(k, 9)
            w_big[j * 128:j * 128 + 64, dz * 128:(dz + 1) * 128] = (
                flipped[k % 2 * 64:k % 2 * 64 + 64].astype(BF16))
            dz, j = divmod(26 - k, 9)
            half = pair if k % 2 else pltpu.roll(pair, 64, 1)
            w_big[j * 128 + 64:(j + 1) * 128, dz * 128:(dz + 1) * 128] = (
                jnp.where(wide_lane >= 64, half, 0.0).astype(BF16))

    t_buf[SLOTS] = jnp.zeros((8, 8, 8, 2 * CH), F32)
    for side in range(2):
        zr[side, SLOTS] = jnp.zeros((64, 2 * CH), BF16)
        yr[side, CAPL] = jnp.zeros((64, 2 * CH), BF16)
        for other in range(2):
            er[side, other, CAPL] = jnp.zeros((8, 2 * CH), F32)

    def clear(z, _):
        d_buf[0, z] = jnp.zeros((18, 8, 2 * CH), F32)
        d_buf[LX + 1, z] = jnp.zeros((18, 8, 2 * CH), F32)
        return 0

    lax.fori_loop(0, 10, clear, 0)

    def inner(b, _):
        for ly in range(YR):
            i = near(1, 1 + ly, b)
            d_buf[b + 1, 1:9, 1 + 8 * ly:9 + 8 * ly] = t_buf[i]
        return 0

    lax.fori_loop(0, LX, inner, 0)

    for m in dirs:
        @pl.when(has(*m))
        def _():
            copies[(-m[0], -m[1])].wait_recv()

    def outer(b, _):
        for zi in range(2):
            for ly in range(YR):
                i = near(2 * zi, 1 + ly, b)
                d_buf[b + 1, 9 * zi, 1 + 8 * ly:9 + 8 * ly] = zr[zi, i].astype(F32).reshape(8, 8, 2 * CH)
            for yi in range(2):
                i = near(2 * zi, 3 * yi, b)
                d_buf[b + 1, 9 * zi, 17 * yi] = er[zi, yi, i]
        for yi in range(2):
            i = near(1, 3 * yi, b)
            d_buf[b + 1, 1:9, 17 * yi] = yr[yi, i].astype(F32).reshape(8, 8, 2 * CH)
        return 0

    lax.fori_loop(0, LX, outer, 0)

    acc[...] = jnp.zeros_like(acc)

    def build(s, c_ref, q, part):
        b = pos[s]
        y0 = s // CAPL * 8
        row = lax.broadcasted_iota(jnp.int32, (10, 8, 2 * CH), 1)
        for z in range(10):
            mid = d_buf[b + 1, z, pl.ds(y0, 10)]
            left = d_buf[b, z, pl.ds(y0, 10)]
            right = d_buf[b + 2, z, pl.ds(y0, 10)]
            shifted = (
                pltpu.roll(jnp.where(row == 7, left, mid), 1, 1),
                mid,
                pltpu.roll(jnp.where(row == 0, right, mid), 7, 1),
            )
            for j in SHIFTS[part]:
                dy, dx = divmod(j, 3)
                c_ref[q, z * 64:(z + 1) * 64, j * 128:(j + 1) * 128] = (
                    shifted[dx][dy:dy + 8].reshape(64, 2 * CH).astype(BF16))

    def terms(s, c_ref, q, part):
        g = g_ref[s].astype(F32) * valid[s]
        wide = jnp.concatenate([g, jnp.zeros((CH, 128), F32)], axis=1)
        lhs = jnp.concatenate([wide, pltpu.roll(wide, 64, 1), pltpu.roll(wide, 128, 1)], axis=0).astype(BF16)
        lo, hi = SHIFTS[part][0] * 128, SHIFTS[part][-1] * 128 + 128
        acc[:, lo:hi] += jnp.dot(lhs, c_ref[q, :, lo:hi], preferred_element_type=F32)

    def all_terms(part):
        build(0, c_even, 0, part)

        def step(q, _):
            terms(2 * q, c_even, q, part)
            build(2 * q + 1, c_odd, q, part)
            terms(2 * q + 1, c_odd, q, part)
            build(jnp.minimum(2 * q + 2, SLOTS - 1), c_even, q + 1, part)
            return 0

        lax.fori_loop(0, SLOTS // 2, step, 0)

    def second_of(s, c_ref, q):
        r = jnp.dot(c_ref[q], w_big[...], preferred_element_type=F32)
        o = (r[0:512, 0:128] + r[64:576, 128:256] + r[128:640, 256:384]) * valid[s]
        ot = o.T
        conv_ref[s] = ot[0:CH].astype(BF16)
        grad_ref[s] = ot[CH:2 * CH].astype(BF16)

    lane = lax.broadcasted_iota(jnp.int32, (CH, 128), 1)
    bufs = ((pay_a, rb1_a, s1_a, rb2_a, f1_a, fb_a), (pay_b, rb1_b, s1_b, rb2_b, f1_b, fb_b))

    def term(k):
        dz, j = divmod(k, 9)
        return acc[dz * 64:(dz + 1) * 64, j * 128:(j + 1) * 128]

    def chunk(part):
        return rows_of(part, n_tile) // n_tile

    def own(part):
        return pl.ds(pl.multiple_of(tile * chunk(part), 8), chunk(part))

    def sum_tile_start(part):
        pay, rb1 = bufs[part][:2]
        used = len(pairs_of(part)) * 64
        for p, (ke, ko) in enumerate(pairs_of(part)):
            odd = jnp.zeros((CH, 128), F32) if ko is None else pltpu.roll(term(ko), 64, 1)
            pay[p * 64:(p + 1) * 64] = jnp.where(lane < 64, term(ke), odd)
        if rows_of(part, n_tile) > used:
            pay[used:] = jnp.zeros((rows_of(part, n_tile) - used, 128), F32)
        started = []
        for d in range(1, n_tile):
            peer = lax.rem(tile + d, n_tile)
            started.append(pltpu.make_async_remote_copy(
                src_ref=pay.at[pl.ds(pl.multiple_of(peer * chunk(part), 8), chunk(part))],
                dst_ref=rb1.at[d], send_sem=tile_s.at[2 * part, d], recv_sem=tile_r.at[2 * part, d],
                device_id=(slab, peer), device_id_type=MESH))
        for c in started:
            c.start()
        return started

    def sum_slab_start(part, before):
        pay, rb1, s1, rb2 = bufs[part][:4]
        for c in before:
            c.wait_recv()
        total = pay[own(part)]
        for d in range(1, n_tile):
            total = total + rb1[d]
        s1[...] = total
        rb2[slab] = total
        started = []
        for d in range(1, n_slab):
            started.append(pltpu.make_async_remote_copy(
                src_ref=s1, dst_ref=rb2.at[slab],
                send_sem=slab_s.at[part, d], recv_sem=slab_r.at[part, d],
                device_id=(lax.rem(slab + d, n_slab), tile), device_id_type=MESH))
        for c in started:
            c.start()
        return started

    def spread_start(part, before):
        rb2, f1, fb = bufs[part][3:]
        for c in before:
            c.wait_recv()
        total = rb2[0]
        for z in range(1, n_slab):
            total = total + rb2[z]
        count = jnp.sum((table_v[...] >= 0).astype(F32), axis=0, keepdims=True)
        count = jnp.sum(jnp.sum(count, axis=2, keepdims=True), axis=1, keepdims=True)[0]
        total = total / jnp.sqrt(count * 512.0)
        f1[...] = total
        fb[own(part)] = total
        started = []
        for d in range(1, n_tile):
            started.append(pltpu.make_async_remote_copy(
                src_ref=f1, dst_ref=fb.at[own(part)],
                send_sem=tile_s.at[2 * part + 1, d], recv_sem=tile_r.at[2 * part + 1, d],
                device_id=(slab, lax.rem(tile + d, n_tile)), device_id_type=MESH))
        for c in started:
            c.start()
        return started

    def finish(part, before):
        fb = bufs[part][5]
        for c in before:
            c.wait_recv()
        for p, (ke, ko) in enumerate(pairs_of(part)):
            both = fb[p * 64:(p + 1) * 64]
            gw_ref[:, ke * 64:ke * 64 + 64] = both[:, 0:64]
            if ko is not None:
                gw_ref[:, ko * 64:ko * 64 + 64] = both[:, 64:128]

    all_terms(0)
    a1 = sum_tile_start(0)
    all_terms(1)
    b1 = sum_tile_start(1)
    second_of(0, c_even, 0)
    a2 = sum_slab_start(0, a1)
    second_of(1, c_odd, 0)
    b2 = sum_slab_start(1, b1)
    second_of(2, c_even, 1)
    second_of(3, c_odd, 1)
    a3 = spread_start(0, a2)
    b3 = spread_start(1, b2)
    second_of(4, c_even, 2)
    second_of(5, c_odd, 2)
    second_of(6, c_even, 3)
    finish(0, a3)
    second_of(7, c_odd, 3)
    finish(1, b3)

    for c in a1 + b1 + a2 + b2 + a3 + b3:
        c.wait_send()
    for m in dirs:
        @pl.when(has(*m))
        def _():
            copies[m].wait_send()


def shards(n_slab, n_tile, features, cotangent, weight, block_table):
    table = jnp.transpose(block_table, (0, 2, 1))
    vmem = pl.BlockSpec(memory_space=pltpu.VMEM)
    smem = pl.BlockSpec(memory_space=pltpu.SMEM)
    dma = pltpu.SemaphoreType.DMA
    sums = []
    for part in range(2):
        rows = rows_of(part, n_tile)
        ch = rows // n_tile
        sums += [
            pltpu.VMEM((rows, 128), F32),
            pltpu.VMEM((n_tile, ch, 128), F32),
            pltpu.VMEM((ch, 128), F32),
            pltpu.VMEM((n_slab, ch, 128), F32),
            pltpu.VMEM((ch, 128), F32),
            pltpu.VMEM((rows, 128), F32),
        ]
    flops = 2 * SLOTS * 640 * 1152 * (384 + 192)
    return pl.pallas_call(
        functools.partial(kernel, n_slab, n_tile),
        out_shape=(
            jax.ShapeDtypeStruct((SLOTS, CH, 512), BF16),
            jax.ShapeDtypeStruct((SLOTS, CH, 512), BF16),
            jax.ShapeDtypeStruct((CH, 27 * CH), F32),
        ),
        in_specs=[smem] + [pl.BlockSpec(memory_space=pl.ANY)] * 4,
        out_specs=(vmem, vmem, vmem),
        scratch_shapes=[
            pltpu.VMEM((SLOTS, CH, 512), BF16),
            pltpu.VMEM((SLOTS, CH, 512), BF16),
            pltpu.VMEM((CH, 27 * CH), BF16),
            pltpu.VMEM(table.shape, jnp.int32),
            dma((4,)),
            pltpu.SMEM((SLOTS,), jnp.int32),
            pltpu.SMEM((SLOTS,), F32),
            pltpu.VMEM((1152, 384), BF16),
            pltpu.VMEM((SLOTS + 1, 8, 8, 8, 128), F32),
            pltpu.VMEM((LX + 2, 10, 18, 8, 128), F32),
            pltpu.VMEM((SLOTS // 2 + 1, 640, 1152), BF16),
            pltpu.VMEM((SLOTS // 2, 640, 1152), BF16),
            pltpu.VMEM((192, 1152), F32),
            pltpu.VMEM((2, SLOTS, 64, 128), BF16),
            pltpu.VMEM((2, SLOTS + 1, 64, 128), BF16),
            pltpu.VMEM((2, CAPL, 64, 128), BF16),
            pltpu.VMEM((2, CAPL + 1, 64, 128), BF16),
            pltpu.VMEM((2, 2, CAPL, 8, 128), F32),
            pltpu.VMEM((2, 2, CAPL + 1, 8, 128), F32),
            *sums,
            dma((8,)), dma((8,)),
            dma((4, n_tile)), dma((4, n_tile)),
            dma((2, n_slab)), dma((2, n_slab)),
        ],
        compiler_params=pltpu.CompilerParams(
            collective_id=0, has_side_effects=True, vmem_limit_bytes=60 * 1024 * 1024
        ),
        cost_estimate=pl.CostEstimate(flops=flops, bytes_accessed=3 << 20, transcendentals=0),
    )(table, features, cotangent, weight, table)


def solution(mesh):
    placed = (P(("slab", "tile"), None, None), P(("slab", "tile"), None, None), P(), P())
    return jax.shard_map(
        functools.partial(shards, mesh.shape["slab"], mesh.shape["tile"]),
        mesh=mesh,
        in_specs=placed,
        out_specs=(P(("slab", "tile"), None, None), P(("slab", "tile"), None, None), P()),
        check_vma=False,
    )
```

```python
import functools

import jax
import jax.numpy as jnp
from jax import lax
from jax.experimental import pallas as pl
from jax.experimental.pallas import tpu as pltpu
from jax.sharding import PartitionSpec as P

LZ = 1
YR = 2
LX = 8
CAPL = 4
CH = 64
SLOTS = LZ * YR * CAPL
PAIRS = 14
SHIFTS = ((0, 1, 2, 3, 4), (5, 6, 7, 8))


def pairs_of(part):
    ks = sorted(9 * dz + j for dz in range(3) for j in SHIFTS[part])
    evens = [k for k in ks if k % 2 == 0]
    odds = [k for k in ks if k % 2]
    return [(k, odds[i] if i < len(odds) else None) for i, k in enumerate(evens)]


def rows_of(part, n_tile):
    unit = 8 * n_tile
    return -(-len(pairs_of(part)) * 64 // unit) * unit

MESH = pl.DeviceIdType.MESH
F32 = jnp.float32
BF16 = jnp.bfloat16


def kernel(n_slab, n_tile,
           table, x_any, g_any, w_any, table_any,
           conv_ref, grad_ref, gw_ref,
           x_ref, g_ref, w_ref, table_v, in_sem, pos, valid, w_big,
           t_buf, d_buf, c_even, c_odd, acc, zs, zr, ys, yr, es, er,
           pay_a, rb1_a, s1_a, rb2_a, f1_a, fb_a,
           pay_b, rb1_b, s1_b, rb2_b, f1_b, fb_b,
           hs_sem, hr_sem, tile_s, tile_r, slab_s, slab_r):
    slab = lax.axis_index("slab")
    tile = lax.axis_index("tile")
    def has(dz, dt):
        ok = None
        for v, d, n in ((slab, dz, n_slab), (tile, dt, n_tile)):
            if d:
                c = (v > 0) if d < 0 else (v < n - 1)
                ok = c if ok is None else jnp.logical_and(ok, c)
        return ok

    loads = [
        pltpu.make_async_copy(src, dst, in_sem.at[i])
        for i, (src, dst) in enumerate(
            ((x_any, x_ref), (g_any, g_ref), (w_any, w_ref), (table_any, table_v)))
    ]
    for c in loads:
        c.start()

    def near(zi, yi, b):
        z = slab + zi - 1
        y = tile * YR + yi - 1
        inside = (z >= 0) & (z < n_slab) & (y >= 0) & (y < n_tile * YR)
        v = table[jnp.clip(z, 0, n_slab - 1), b, jnp.clip(y, 0, n_tile * YR - 1)]
        none = CAPL if yi in (0, YR + 1) else SLOTS
        return jnp.where(inside & (v >= 0), jnp.maximum(v - (CAPL if yi == 0 else 0), 0), none)

    barrier = pltpu.get_barrier_semaphore()
    for d in range(1, n_tile):
        pl.semaphore_signal(barrier, inc=1, device_id=(slab, lax.rem(tile + d, n_tile)), device_id_type=MESH)
    for d in range(1, n_slab):
        pl.semaphore_signal(barrier, inc=1, device_id=(lax.rem(slab + d, n_slab), tile), device_id_type=MESH)
    diagonals = [(dz, dt) for dz in (-1, 1) for dt in (-1, 1)]
    for dz, dt in diagonals:
        @pl.when(has(dz, dt))
        def _():
            pl.semaphore_signal(barrier, inc=1, device_id=(slab + dz, tile + dt), device_id_type=MESH)

    def to_rows(s, y_side):
        both = jnp.concatenate([x_ref[s].astype(F32), g_ref[s].astype(F32)], axis=0)
        r = both.T
        r4 = r.reshape(8, 8, 8, 2 * CH)
        t_buf[s] = r4
        zs[0, s] = r[0:64].astype(BF16)
        zs[1, s] = r[448:512].astype(BF16)
        yrow = 0 if y_side == 0 else 7
        q = s - CAPL * y_side
        ys[y_side, q] = r4[:, yrow].reshape(64, 2 * CH).astype(BF16)
        es[0, y_side, q] = r4[0, yrow]
        es[1, y_side, q] = r4[7, yrow]

    for c in loads[:2]:
        c.wait()
    for s in range(SLOTS):
        to_rows(s, s // CAPL)

    z_near = (slab > 0).astype(jnp.int32) + (slab < n_slab - 1).astype(jnp.int32)
    t_near = (tile > 0).astype(jnp.int32) + (tile < n_tile - 1).astype(jnp.int32)
    pl.semaphore_wait(barrier, n_tile - 1 + n_slab - 1 + z_near * t_near)

    dirs = [(dz, dt) for dz in (-1, 0, 1) for dt in (-1, 0, 1) if dz or dt]
    copies = {}
    for m, (dz, dt) in enumerate(dirs):
        zi, yi = (dz + 1) // 2, (dt + 1) // 2
        if dt == 0:
            src, dst = zs.at[zi], zr.at[1 - zi, pl.ds(0, SLOTS)]
        elif dz == 0:
            src, dst = ys.at[yi], yr.at[1 - yi, pl.ds(0, CAPL)]
        else:
            src, dst = es.at[zi, yi], er.at[1 - zi, 1 - yi, pl.ds(0, CAPL)]
        copies[(dz, dt)] = pltpu.make_async_remote_copy(
            src_ref=src, dst_ref=dst, send_sem=hs_sem.at[m], recv_sem=hr_sem.at[7 - m],
            device_id=(slab + dz, tile + dt), device_id_type=MESH)
    for m in dirs:
        @pl.when(has(*m))
        def _():
            copies[m].start()

    for s in range(SLOTS):
        at, found = jnp.int32(0), jnp.float32(0)
        for b in range(LX):
            hit = table[slab, b, tile * YR + s // CAPL] == s
            at = jnp.where(hit, b, at)
            found = jnp.where(hit, 1.0, found)
        pos[s] = at
        valid[s] = found

    for c in loads[2:]:
        c.wait()
    wide_lane = lax.broadcasted_iota(jnp.int32, (CH, 128), 1)
    for p in range(PAIRS):
        if p < PAIRS - 1:
            pair = w_ref[:, p * 128:(p + 1) * 128].astype(F32)
        else:
            pair = jnp.concatenate(
                [w_ref[:, p * 128:27 * CH].astype(F32), jnp.zeros((CH, 64), F32)], axis=1)
        flipped = jnp.concatenate([pair, jnp.zeros((CH, 128), F32)], axis=0).T
        for k in (2 * p, 2 * p + 1):
            if k >= 27:
                continue
            dz, j = divmod(k, 9)
            w_big[j * 128:j * 128 + 64, dz * 128:(dz + 1) * 128] = (
                flipped[k % 2 * 64:k % 2 * 64 + 64].astype(BF16))
            dz, j = divmod(26 - k, 9)
            half = pair if k % 2 else pltpu.roll(pair, 64, 1)
            w_big[j * 128 + 64:(j + 1) * 128, dz * 128:(dz + 1) * 128] = (
                jnp.where(wide_lane >= 64, half, 0.0).astype(BF16))

    t_buf[SLOTS] = jnp.zeros((8, 8, 8, 2 * CH), F32)
    for side in range(2):
        zr[side, SLOTS] = jnp.zeros((64, 2 * CH), BF16)
        yr[side, CAPL] = jnp.zeros((64, 2 * CH), BF16)
        for other in range(2):
            er[side, other, CAPL] = jnp.zeros((8, 2 * CH), F32)

    def clear(z, _):
        d_buf[0, z] = jnp.zeros((18, 8, 2 * CH), F32)
        d_buf[LX + 1, z] = jnp.zeros((18, 8, 2 * CH), F32)
        return 0

    lax.fori_loop(0, 10, clear, 0)

    def inner(b, _):
        for ly in range(YR):
            i = near(1, 1 + ly, b)
            d_buf[b + 1, 1:9, 1 + 8 * ly:9 + 8 * ly] = t_buf[i]
        return 0

    lax.fori_loop(0, LX, inner, 0)

    for m in dirs:
        @pl.when(has(*m))
        def _():
            copies[(-m[0], -m[1])].wait_recv()

    def outer(b, _):
        for zi in range(2):
            for ly in range(YR):
                i = near(2 * zi, 1 + ly, b)
                d_buf[b + 1, 9 * zi, 1 + 8 * ly:9 + 8 * ly] = zr[zi, i].astype(F32).reshape(8, 8, 2 * CH)
            for yi in range(2):
                i = near(2 * zi, 3 * yi, b)
                d_buf[b + 1, 9 * zi, 17 * yi] = er[zi, yi, i]
        for yi in range(2):
            i = near(1, 3 * yi, b)
            d_buf[b + 1, 1:9, 17 * yi] = yr[yi, i].astype(F32).reshape(8, 8, 2 * CH)
        return 0

    lax.fori_loop(0, LX, outer, 0)

    acc[...] = jnp.zeros_like(acc)

    def build(s, c_ref, q, part):
        b = pos[s]
        y0 = s // CAPL * 8
        row = lax.broadcasted_iota(jnp.int32, (10, 8, 2 * CH), 1)
        for z in range(10):
            mid = d_buf[b + 1, z, pl.ds(y0, 10)]
            left = d_buf[b, z, pl.ds(y0, 10)]
            right = d_buf[b + 2, z, pl.ds(y0, 10)]
            shifted = (
                pltpu.roll(jnp.where(row == 7, left, mid), 1, 1),
                mid,
                pltpu.roll(jnp.where(row == 0, right, mid), 7, 1),
            )
            for j in SHIFTS[part]:
                dy, dx = divmod(j, 3)
                c_ref[q, z * 64:(z + 1) * 64, j * 128:(j + 1) * 128] = (
                    shifted[dx][dy:dy + 8].reshape(64, 2 * CH).astype(BF16))

    def terms(s, c_ref, q, part):
        g = g_ref[s].astype(F32) * valid[s]
        wide = jnp.concatenate([g, jnp.zeros((CH, 128), F32)], axis=1)
        lhs = jnp.concatenate([wide, pltpu.roll(wide, 64, 1), pltpu.roll(wide, 128, 1)], axis=0).astype(BF16)
        lo, hi = SHIFTS[part][0] * 128, SHIFTS[part][-1] * 128 + 128
        acc[:, lo:hi] += jnp.dot(lhs, c_ref[q, :, lo:hi], preferred_element_type=F32)

    def all_terms(part):
        build(0, c_even, 0, part)

        def step(q, _):
            terms(2 * q, c_even, q, part)
            build(2 * q + 1, c_odd, q, part)
            terms(2 * q + 1, c_odd, q, part)
            build(jnp.minimum(2 * q + 2, SLOTS - 1), c_even, q + 1, part)
            return 0

        lax.fori_loop(0, SLOTS // 2, step, 0)

    def second_of(s, c_ref, q):
        r = jnp.dot(c_ref[q], w_big[...], preferred_element_type=F32)
        o = (r[0:512, 0:128] + r[64:576, 128:256] + r[128:640, 256:384]) * valid[s]
        ot = o.T
        conv_ref[s] = ot[0:CH].astype(BF16)
        grad_ref[s] = ot[CH:2 * CH].astype(BF16)

    lane = lax.broadcasted_iota(jnp.int32, (CH, 128), 1)
    bufs = ((pay_a, rb1_a, s1_a, rb2_a, f1_a, fb_a), (pay_b, rb1_b, s1_b, rb2_b, f1_b, fb_b))

    def term(k):
        dz, j = divmod(k, 9)
        return acc[dz * 64:(dz + 1) * 64, j * 128:(j + 1) * 128]

    def chunk(part):
        return rows_of(part, n_tile) // n_tile

    def own(part):
        return pl.ds(pl.multiple_of(tile * chunk(part), 8), chunk(part))

    def sum_tile_start(part):
        pay, rb1 = bufs[part][:2]
        used = len(pairs_of(part)) * 64
        for p, (ke, ko) in enumerate(pairs_of(part)):
            odd = jnp.zeros((CH, 128), F32) if ko is None else pltpu.roll(term(ko), 64, 1)
            pay[p * 64:(p + 1) * 64] = jnp.where(lane < 64, term(ke), odd)
        if rows_of(part, n_tile) > used:
            pay[used:] = jnp.zeros((rows_of(part, n_tile) - used, 128), F32)
        started = []
        for d in range(1, n_tile):
            peer = lax.rem(tile + d, n_tile)
            started.append(pltpu.make_async_remote_copy(
                src_ref=pay.at[pl.ds(pl.multiple_of(peer * chunk(part), 8), chunk(part))],
                dst_ref=rb1.at[d], send_sem=tile_s.at[2 * part, d], recv_sem=tile_r.at[2 * part, d],
                device_id=(slab, peer), device_id_type=MESH))
        for c in started:
            c.start()
        return started

    def slab_copies(part):
        s1, rb2 = bufs[part][2:4]
        return [pltpu.make_async_remote_copy(
            src_ref=s1, dst_ref=rb2.at[slab],
            send_sem=slab_s.at[part, d], recv_sem=slab_r.at[part, d],
            device_id=(lax.rem(slab + d, n_slab), tile), device_id_type=MESH) for d in range(1, n_slab)]

    def spread_copies(part):
        f1, fb = bufs[part][4:]
        return [pltpu.make_async_remote_copy(
            src_ref=f1, dst_ref=fb.at[own(part)],
            send_sem=tile_s.at[2 * part + 1, d], recv_sem=tile_r.at[2 * part + 1, d],
            device_id=(slab, lax.rem(tile + d, n_tile)), device_id_type=MESH) for d in range(1, n_tile)]

    def sum_slab(part, before, started):
        pay, rb1, s1, rb2 = bufs[part][:4]
        for c in before:
            c.wait_recv()
        total = pay[own(part)]
        for d in range(1, n_tile):
            total = total + rb1[d]
        s1[...] = total
        rb2[slab] = total
        for c in started:
            c.start()

    def spread(part, before, started):
        rb2, f1, fb = bufs[part][3:]
        for c in before:
            c.wait_recv()
        total = rb2[0]
        for z in range(1, n_slab):
            total = total + rb2[z]
        count = jnp.sum((table_v[...] >= 0).astype(F32), axis=0, keepdims=True)
        count = jnp.sum(jnp.sum(count, axis=2, keepdims=True), axis=1, keepdims=True)[0]
        total = total / jnp.sqrt(count * 512.0)
        f1[...] = total
        fb[own(part)] = total
        for c in started:
            c.start()

    def finish(part, before):
        fb = bufs[part][5]
        for c in before:
            c.wait_recv()
        for p, (ke, ko) in enumerate(pairs_of(part)):
            both = fb[p * 64:(p + 1) * 64]
            gw_ref[:, ke * 64:ke * 64 + 64] = both[:, 0:64]
            if ko is not None:
                gw_ref[:, ko * 64:ko * 64 + 64] = both[:, 64:128]

    all_terms(0)
    a1 = sum_tile_start(0)
    all_terms(1)
    b1 = sum_tile_start(1)
    a2, b2, a3, b3 = slab_copies(0), slab_copies(1), spread_copies(0), spread_copies(1)

    def outputs(q, _):
        second_of(2 * q, c_even, q)
        second_of(2 * q + 1, c_odd, q)

        @pl.when(q == 0)
        def _():
            sum_slab(0, a1, a2)
            sum_slab(1, b1, b2)

        @pl.when(q == 1)
        def _():
            spread(0, a2, a3)
            spread(1, b2, b3)
        return 0

    lax.fori_loop(0, SLOTS // 2, outputs, 0)
    finish(0, a3)
    finish(1, b3)

    for c in a1 + b1 + a2 + b2 + a3 + b3:
        c.wait_send()
    for m in dirs:
        @pl.when(has(*m))
        def _():
            copies[m].wait_send()


def shards(n_slab, n_tile, features, cotangent, weight, block_table):
    table = jnp.transpose(block_table, (0, 2, 1))
    vmem = pl.BlockSpec(memory_space=pltpu.VMEM)
    smem = pl.BlockSpec(memory_space=pltpu.SMEM)
    dma = pltpu.SemaphoreType.DMA
    sums = []
    for part in range(2):
        rows = rows_of(part, n_tile)
        ch = rows // n_tile
        sums += [
            pltpu.VMEM((rows, 128), F32),
            pltpu.VMEM((n_tile, ch, 128), F32),
            pltpu.VMEM((ch, 128), F32),
            pltpu.VMEM((n_slab, ch, 128), F32),
            pltpu.VMEM((ch, 128), F32),
            pltpu.VMEM((rows, 128), F32),
        ]
    flops = 2 * SLOTS * 640 * 1152 * (384 + 192)
    return pl.pallas_call(
        functools.partial(kernel, n_slab, n_tile),
        out_shape=(
            jax.ShapeDtypeStruct((SLOTS, CH, 512), BF16),
            jax.ShapeDtypeStruct((SLOTS, CH, 512), BF16),
            jax.ShapeDtypeStruct((CH, 27 * CH), F32),
        ),
        in_specs=[smem] + [pl.BlockSpec(memory_space=pl.ANY)] * 4,
        out_specs=(vmem, vmem, vmem),
        scratch_shapes=[
            pltpu.VMEM((SLOTS, CH, 512), BF16),
            pltpu.VMEM((SLOTS, CH, 512), BF16),
            pltpu.VMEM((CH, 27 * CH), BF16),
            pltpu.VMEM(table.shape, jnp.int32),
            dma((4,)),
            pltpu.SMEM((SLOTS,), jnp.int32),
            pltpu.SMEM((SLOTS,), F32),
            pltpu.VMEM((1152, 384), BF16),
            pltpu.VMEM((SLOTS + 1, 8, 8, 8, 128), F32),
            pltpu.VMEM((LX + 2, 10, 18, 8, 128), F32),
            pltpu.VMEM((SLOTS // 2 + 1, 640, 1152), BF16),
            pltpu.VMEM((SLOTS // 2, 640, 1152), BF16),
            pltpu.VMEM((192, 1152), F32),
            pltpu.VMEM((2, SLOTS, 64, 128), BF16),
            pltpu.VMEM((2, SLOTS + 1, 64, 128), BF16),
            pltpu.VMEM((2, CAPL, 64, 128), BF16),
            pltpu.VMEM((2, CAPL + 1, 64, 128), BF16),
            pltpu.VMEM((2, 2, CAPL, 8, 128), F32),
            pltpu.VMEM((2, 2, CAPL + 1, 8, 128), F32),
            *sums,
            dma((8,)), dma((8,)),
            dma((4, n_tile)), dma((4, n_tile)),
            dma((2, n_slab)), dma((2, n_slab)),
        ],
        compiler_params=pltpu.CompilerParams(
            collective_id=0, has_side_effects=True, vmem_limit_bytes=60 * 1024 * 1024
        ),
        cost_estimate=pl.CostEstimate(flops=flops, bytes_accessed=3 << 20, transcendentals=0),
    )(table, features, cotangent, weight, table)


def solution(mesh):
    placed = (P(("slab", "tile"), None, None), P(("slab", "tile"), None, None), P(), P())
    return jax.shard_map(
        functools.partial(shards, mesh.shape["slab"], mesh.shape["tile"]),
        mesh=mesh,
        in_specs=placed,
        out_specs=(P(("slab", "tile"), None, None), P(("slab", "tile"), None, None), P()),
        check_vma=False,
    )
```
